512 devices in a mesh: pair: 64 (over z, x), day: 8 (over y, core).
Axes of the slice: x: 4, y: 4, z: 16, core: 2. Of those that a mesh axis runs over, the one named last changes fastest.
Arguments:
- spectra: float32 [8, 4096, 4096], P('day', 'pair'), may hold values from -6 to 6
- station_pairs: int32 [16384, 2], P('pair'), may hold values from 0 to 4095, as said below
- station_home: int32 [4096], replicated, may hold values from 0 to 4095, as said below
- block_lists: int32 [64, 64, 8], replicated, may hold values from -1 to 63, as said below
Outputs:
- stacked: float32 [16384, 256], P(('pair', 'day'))
The draws below stay inside these ranges and needn't reach their ends.
Inputs may be any that keep to these rules, and one draw needn't show every extreme that they name: `station_home`: A permutation: each station has its own stored row. `station_pairs`: the two stations of a pair differ. `block_lists`: entry [o, s, k] is a row within station block s (stored rows s * 64 to (s + 1) * 64 - 1) or -1; the valid entries of [o, s] are distinct and come first, at least one. Every pair block has some station block with all 8 slots valid, and some pair block has all slots valid from every station block.
All inputs are finite; a program needn't handle non-finite values.
Results may differ from the reference program's by a relative error of at most 0.015.
Values may be sent and summed in bfloat16 or wider, within the bound.
No kernel may reach another device: no remote copies, remote signals or barrier semaphores. Data moves between devices by JAX's collectives and lax.ppermute only.
A program may use at most 64 MiB of HBM per device.

```python
import math
import jax
import jax.numpy as jnp
from jax import lax

S_DEV = 64
P_DEV = 256
FREQS = 2048
LAGS = 256
HALF = 32
BLOCKS = 64
CAP = 8
STATIONS = 4096
PAIRS = 16384
DAYS = 8


def layout(key):
    folded = jax.random.fold_in(key, 11)
    subkeys = jax.random.split(folded, 8)
    station_ids = jax.random.permutation(subkeys[0], STATIONS).astype(jnp.int32)
    station_home = jnp.argsort(station_ids).astype(jnp.int32)
    counts = jax.random.randint(subkeys[1], (BLOCKS, BLOCKS), 1, CAP + 1)
    hottest = jax.random.randint(subkeys[2], (BLOCKS, 1), 0, BLOCKS)
    fullest = jax.random.randint(subkeys[3], (), 0, BLOCKS)
    source_column = jnp.arange(BLOCKS, dtype=jnp.int32)[None, :]
    owner_column = jnp.arange(BLOCKS, dtype=jnp.int32)[:, None]
    counts = jnp.where(source_column == hottest, CAP, counts)
    counts = jnp.where(owner_column == fullest, CAP, counts)
    scores = jax.random.randint(subkeys[4], (BLOCKS, BLOCKS, S_DEV), 0, 1 << 20) * S_DEV + jnp.arange(S_DEV, dtype=jnp.int32)
    row_order = jnp.argsort(scores, axis=2)[:, :, :CAP].astype(jnp.int32)
    slot_index = jnp.arange(CAP, dtype=jnp.int32)
    block_lists = jnp.where(slot_index[None, None, :] < counts[:, :, None], row_order, -1).astype(jnp.int32)
    used_rows = jnp.take_along_axis(row_order, slot_index[None, None, :] % counts[:, :, None], axis=2)
    stored_rows = jnp.arange(BLOCKS, dtype=jnp.int32)[None, :, None] * S_DEV + used_rows
    slot_stations = jnp.take(station_ids, stored_rows, axis=0)
    source_scores = jax.random.randint(subkeys[5], (BLOCKS, BLOCKS), 0, 1 << 20) * BLOCKS + jnp.arange(BLOCKS, dtype=jnp.int32)
    source_order = jnp.argsort(source_scores, axis=1)
    arranged = jnp.take_along_axis(slot_stations, source_order[:, :, None], axis=1).reshape(BLOCKS, BLOCKS * CAP)
    first_end = arranged[:, :P_DEV]
    second_end = arranged[:, P_DEV:]
    pair_scores = jax.random.randint(subkeys[6], (BLOCKS, P_DEV), 0, 1 << 20) * P_DEV + jnp.arange(P_DEV, dtype=jnp.int32)
    pair_order = jnp.argsort(pair_scores, axis=1)
    first_end = jnp.take_along_axis(first_end, pair_order, axis=1)
    second_end = jnp.take_along_axis(second_end, pair_order, axis=1)
    flipped = jax.random.randint(subkeys[7], (BLOCKS, P_DEV), 0, 2) == 1
    left_station = jnp.where(flipped, second_end, first_end)
    right_station = jnp.where(flipped, first_end, second_end)
    station_pairs = jnp.stack([left_station, right_station], axis=-1).reshape(PAIRS, 2).astype(jnp.int32)
    return (station_pairs, station_home, block_lists)


def draw_station_pairs(key, part):
    return layout(key)[0]


def draw_station_home(key, part):
    return layout(key)[1]


def draw_block_lists(key, part):
    return layout(key)[2]


def level_of(rng, shape, shards, least, top_value):
    gain, own = 1.0, jax.random.fold_in(rng, 6)
    for axis_at, parts in shards:
        draws = jnp.exp(jax.random.uniform(jax.random.fold_in(own, axis_at), (parts,), jnp.float32, least / len(shards), top_value / len(shards)))
        gain = gain * jnp.repeat(draws, shape[axis_at] // parts).reshape([-1 if axis == axis_at else 1 for axis in range(len(shape))])
    return gain


def normal_values(own_key, dims, spread, limit, cuts=(), kind=jnp.bfloat16):
    factor_of = level_of(own_key, dims, cuts, -0.22, 0.18) if cuts else 1.0
    entries = jax.random.normal(own_key, dims, jnp.float32) * spread * factor_of
    return jnp.minimum(jnp.maximum(entries, -limit), limit).astype(kind)


def setup_inputs(seed: int = 0) -> dict:
    keys = jax.random.split(jax.random.key(seed), 5)
    spectra = normal_values(keys[0], (DAYS, STATIONS, 2 * FREQS), 1.0, 6.0, ((0, 8), (1, 64)), jnp.float32)
    station_pairs = draw_station_pairs(jax.random.fold_in(keys[4], 71), 0)
    station_home = draw_station_home(jax.random.fold_in(keys[4], 71), 0)
    block_lists = draw_block_lists(jax.random.fold_in(keys[4], 71), 0)
    return dict(spectra=spectra, station_pairs=station_pairs, station_home=station_home, block_lists=block_lists)


def lag_basis():
    freq_index = jnp.arange(FREQS, dtype=jnp.int32)
    lag_index = jnp.arange(LAGS, dtype=jnp.int32) - LAGS // 2
    phase_steps = jnp.mod(freq_index[:, None] * lag_index[None, :], 2 * FREQS)
    angles = phase_steps.astype(jnp.float32) * (2.0 * math.pi / (2 * FREQS))
    scaling = 1.0 / math.sqrt(FREQS)
    return jnp.concatenate([jnp.cos(angles) * scaling, -jnp.sin(angles) * scaling], axis=0).astype(jnp.bfloat16)

def whiten(station_rows):
    real_part = station_rows[:, :FREQS]
    imag_part = station_rows[:, FREQS:]
    amplitude = jnp.sqrt(real_part * real_part + imag_part * imag_part)
    running = jnp.zeros_like(amplitude)
    for offset in range(-HALF, HALF + 1):
        running = running + jnp.roll(amplitude, offset, axis=1)
    denominator = running / (2 * HALF + 1) + 1e-05
    return jnp.concatenate([real_part / denominator, imag_part / denominator], axis=1).astype(jnp.bfloat16)

def cross_spectra(first_end, second_end):
    first_real = first_end[:, :FREQS].astype(jnp.float32)
    first_imag = first_end[:, FREQS:].astype(jnp.float32)
    second_real = second_end[:, :FREQS].astype(jnp.float32)
    second_imag = second_end[:, FREQS:].astype(jnp.float32)
    real_cross = first_real * second_real + first_imag * second_imag
    imag_cross = first_imag * second_real - first_real * second_imag
    return jnp.concatenate([real_cross, imag_cross], axis=1).astype(jnp.bfloat16)

def reference(spectra, station_pairs, station_home, block_lists):
    basis = lag_basis().astype(jnp.float32)
    storage = jnp.take(station_home, station_pairs, axis=0).astype(jnp.int32)
    owner_block = (jnp.arange(PAIRS, dtype=jnp.int32) // P_DEV)[:, None]
    list_index = (owner_block * BLOCKS + storage // S_DEV).astype(jnp.int32)
    flat_lists = block_lists.reshape(BLOCKS * BLOCKS, CAP)
    candidates = jnp.take(flat_lists, list_index, axis=0)
    listed = jnp.any(candidates == (storage % S_DEV)[:, :, None], axis=2)

    def one_day(accumulated, day_spectra):
        whitened = whiten(day_spectra)
        zero_row = jnp.zeros((), jnp.bfloat16)
        first_end = jnp.where(listed[:, 0:1], jnp.take(whitened, storage[:, 0], axis=0), zero_row)
        second_end = jnp.where(listed[:, 1:2], jnp.take(whitened, storage[:, 1], axis=0), zero_row)
        cross = cross_spectra(first_end, second_end).astype(jnp.float32)
        corr_day = jnp.dot(cross, basis, precision=lax.Precision.HIGHEST, preferred_element_type=jnp.float32)
        return (accumulated + corr_day, None)
    stacked, ignored = lax.scan(one_day, jnp.zeros((PAIRS, LAGS), jnp.float32), spectra)
    return stacked / math.sqrt(DAYS)
```

```python
import functools
import math

import jax
import jax.numpy as jnp
from jax import lax
from jax.experimental import pallas as pl
from jax.experimental.pallas import tpu as pltpu
from jax.sharding import Mesh
from jax.sharding import PartitionSpec as P

HALF = 32
LAGS = 256
LANES = 128


def basis_slice(first, count, freqs):
    freq_index = first + jnp.arange(count, dtype=jnp.int32)
    lag_index = jnp.arange(LAGS, dtype=jnp.int32) - LAGS // 2
    phase_steps = jnp.mod(freq_index[:, None] * lag_index[None, :], 2 * freqs)
    angles = phase_steps.astype(jnp.float32) * (2.0 * math.pi / (2 * freqs))
    scaling = 1.0 / math.sqrt(freqs)
    return jnp.concatenate([jnp.cos(angles) * scaling, -jnp.sin(angles) * scaling], axis=0).astype(
        jnp.bfloat16
    )


def whiten(station_rows):
    row_count = station_rows.shape[0]
    freq_count = station_rows.shape[1] // 2
    real_part = station_rows[:, :freq_count]
    imag_part = station_rows[:, freq_count:]
    amplitude = jnp.sqrt(real_part * real_part + imag_part * imag_part)
    extended = jnp.concatenate(
        [amplitude[:, freq_count - LANES :], amplitude, amplitude[:, :LANES]], axis=1
    )
    tile_count = freq_count // LANES
    grouped = extended.reshape(row_count, tile_count + 2, LANES)
    windows = jnp.concatenate(
        [grouped[:, :tile_count], grouped[:, 1 : tile_count + 1], grouped[:, 2:]], axis=2
    )
    band_rows = jnp.arange(3 * LANES, dtype=jnp.int32)[:, None]
    band_cols = jnp.arange(LANES, dtype=jnp.int32)[None, :]
    band_matrix = (jnp.abs(band_rows - band_cols - LANES) <= HALF).astype(jnp.float32)
    running = jnp.einsum(
        "snu,uv->snv", windows, band_matrix, precision=lax.Precision.HIGHEST
    ).reshape(row_count, freq_count)
    denominator = running / (2 * HALF + 1) + 1e-05
    return (real_part / denominator).astype(jnp.bfloat16), (imag_part / denominator).astype(
        jnp.bfloat16
    )


def correlate_kernel(count, index_ref, *refs):
    blocks = refs[:count]
    basis_ref, out_ref, table, cross, sems = refs[count:]
    block_rows = blocks[0].shape[0]
    pair_count = out_ref.shape[0]
    copies = [
        pltpu.make_async_copy(
            blocks[k], table.at[pl.ds(k * block_rows, block_rows)], sems.at[k]
        )
        for k in range(count)
    ]
    for copy in copies:
        copy.start()
    zero_rows = table.shape[0] - count * block_rows
    table[pl.ds(count * block_rows, zero_rows)] = jnp.zeros((zero_rows, 8, LANES), table.dtype)
    for copy in copies:
        copy.wait()
    low = lax.broadcasted_iota(jnp.int32, (8, LANES), 0) < 4

    group = 8

    def one_group(g, carry):
        for u in range(group):
            p = g * group + u
            a = table[index_ref[0, p]].astype(jnp.float32)
            b = table[index_ref[1, p]].astype(jnp.float32)
            straight = a * b
            crossed = a * pltpu.roll(b, 4, 0)
            real_cross = straight + pltpu.roll(straight, 4, 0)
            imag_cross = crossed - pltpu.roll(crossed, 4, 0)
            start = pl.multiple_of(p * 8, 8)
            cross[pl.ds(start, 8), :] = jnp.where(low, real_cross, imag_cross)
        return carry

    lax.fori_loop(0, pair_count // group, one_group, 0)
    step = 256

    def one_dot(i, carry):
        start = pl.multiple_of(i * step * 8, step * 8)
        rows = jnp.concatenate(
            [
                cross[pl.ds(start + k, step, stride=8), :].astype(jnp.bfloat16)
                for k in range(8)
            ],
            axis=1,
        )
        product = jnp.dot(rows, basis_ref[...], preferred_element_type=jnp.float32)
        out_ref[pl.ds(pl.multiple_of(i * step, step), step), :] = product.astype(out_ref.dtype)
        return carry

    lax.fori_loop(0, pair_count // step, one_dot, 0)


def correlate(index, blocks, basis):
    count = len(blocks)
    block_rows = blocks[0].shape[0]
    pair_count = index.shape[1]
    vmem = pl.BlockSpec(memory_space=pltpu.VMEM)
    return pl.pallas_call(
        functools.partial(correlate_kernel, count),
        out_shape=jax.ShapeDtypeStruct((pair_count, LAGS), jnp.bfloat16),
        in_specs=[pl.BlockSpec(memory_space=pltpu.SMEM)]
        + [pl.BlockSpec(memory_space=pl.ANY)] * count
        + [vmem],
        out_specs=vmem,
        scratch_shapes=[
            pltpu.VMEM((count * block_rows + 8, 8, LANES), jnp.bfloat16),
            pltpu.VMEM((pair_count * 8, LANES), jnp.float32),
            pltpu.SemaphoreType.DMA((count,)),
        ],
        compiler_params=pltpu.CompilerParams(vmem_limit_bytes=36 * 1024 * 1024),
    )(index, *blocks, basis)


def ring(block, axis):
    size = lax.axis_size(axis)
    up = [(i, (i + 1) % size) for i in range(size)]
    down = [(i, (i - 1) % size) for i in range(size)]
    gathered = [None] * size
    gathered[0] = block
    from_below = from_above = block
    for step in range(1, size // 2 + 1):
        from_below = lax.ppermute(from_below, axis, up)
        gathered[size - step] = from_below
        if step < size - step:
            from_above = lax.ppermute(from_above, axis, down)
            gathered[step] = from_above
    return gathered


def pick(table, digits_high, digits_low):
    rows, cols = table.shape
    hot = (digits_high[:, None] == jnp.arange(rows, dtype=jnp.int32)[None, :]).astype(jnp.bfloat16)
    digits = jnp.concatenate([table // 64, table % 64], axis=1).astype(jnp.bfloat16)
    found = jnp.dot(hot, digits, preferred_element_type=jnp.float32)
    mask = digits_low[:, None] == jnp.arange(cols, dtype=jnp.int32)[None, :]
    high = jnp.sum(jnp.where(mask, found[:, :cols], 0.0), axis=1)
    low = jnp.sum(jnp.where(mask, found[:, cols:], 0.0), axis=1)
    return (high * 64.0 + low).astype(jnp.int32)


def body(spectra, station_pairs, station_home, block_lists):
    xs, ys, cs, zs = (lax.axis_size(n) for n in ("x", "y", "c", "z"))
    z, x = lax.axis_index("z"), lax.axis_index("x")
    owner = z * xs + x
    rows = spectra.shape[1]
    freqs = spectra.shape[2] // 2
    share = freqs // xs
    day_count = spectra.shape[0] * ys * cs
    pair_slots = station_pairs.shape[0]
    station_count = station_home.shape[0]

    ends = jnp.concatenate([station_pairs[:, 0], station_pairs[:, 1]], axis=0)
    storage = pick(station_home.reshape(64, station_count // 64), ends // 64, ends % 64)
    source_block = storage // rows
    source_row = storage % rows
    wanted = lax.dynamic_index_in_dim(block_lists, owner, 0, keepdims=False)
    hot = (source_block[:, None] == jnp.arange(wanted.shape[0], dtype=jnp.int32)[None, :]).astype(
        jnp.bfloat16
    )
    candidates = jnp.dot(hot, wanted.astype(jnp.bfloat16), preferred_element_type=jnp.float32)
    listed = jnp.any(candidates == source_row.astype(jnp.float32)[:, None], axis=1)
    plane_rows = rows * xs
    ahead = jnp.mod(storage // plane_rows - z, zs)
    place = jnp.where(listed, ahead * plane_rows + storage % plane_rows, zs * plane_rows)
    place = jnp.broadcast_to(place.reshape(1, 4, LANES), (xs, 4, LANES))
    places = lax.all_to_all(place, "x", 0, 0, tiled=True).reshape(xs, 2, pair_slots)
    index = places.transpose(1, 0, 2).reshape(2, xs * pair_slots)

    real_part, imag_part = whiten(spectra[0])
    outbound = jnp.concatenate(
        [
            real_part.reshape(rows, xs, share // LANES, LANES),
            imag_part.reshape(rows, xs, share // LANES, LANES),
        ],
        axis=2,
    ).transpose(1, 0, 2, 3)
    block = lax.all_to_all(outbound, "x", 0, 0, tiled=True).reshape(plane_rows, 8, LANES)
    blocks = ring(block, "z")
    partial = correlate(index, blocks, basis_slice(x * share, share, freqs))

    group = xs * ys * cs
    slots = xs * pair_slots // group
    shares = lax.all_to_all(
        partial.reshape(group, slots, LAGS), ("x", "y", "c"), 0, 0, tiled=True
    )
    return jnp.sum(shares.astype(jnp.float32), axis=0) / math.sqrt(day_count)


def solution(mesh):
    inner = Mesh(mesh.devices.reshape(16, 4, 4, 2), ("z", "x", "y", "c"))
    in_specs = (P(("y", "c"), ("z", "x"), None), P(("z", "x"), None), P(), P())
    out_specs = P(("z", "x", "y", "c"), None)
    return jax.shard_map(
        body, mesh=inner, in_specs=in_specs, out_specs=out_specs, check_vma=False
    )
```

```python
import functools
import math

import jax
import jax.numpy as jnp
from jax import lax
from jax.experimental import pallas as pl
from jax.experimental.pallas import tpu as pltpu
from jax.sharding import Mesh
from jax.sharding import PartitionSpec as P

HALF = 32
LAGS = 256
LANES = 128


def basis_slice(first, count, freqs):
    freq_index = first + jnp.arange(count, dtype=jnp.int32)
    lag_index = jnp.arange(LAGS, dtype=jnp.int32) - LAGS // 2
    phase_steps = jnp.mod(freq_index[:, None] * lag_index[None, :], 2 * freqs)
    angles = phase_steps.astype(jnp.float32) * (2.0 * math.pi / (2 * freqs))
    scaling = 1.0 / math.sqrt(freqs)
    return jnp.concatenate([jnp.cos(angles) * scaling, -jnp.sin(angles) * scaling], axis=0).astype(
        jnp.bfloat16
    )


def whiten(station_rows):
    row_count = station_rows.shape[0]
    freq_count = station_rows.shape[1] // 2
    real_part = station_rows[:, :freq_count]
    imag_part = station_rows[:, freq_count:]
    amplitude = jnp.sqrt(real_part * real_part + imag_part * imag_part)
    extended = jnp.concatenate(
        [amplitude[:, freq_count - LANES :], amplitude, amplitude[:, :LANES]], axis=1
    )
    tile_count = freq_count // LANES
    grouped = extended.reshape(row_count, tile_count + 2, LANES)
    windows = jnp.concatenate(
        [grouped[:, :tile_count], grouped[:, 1 : tile_count + 1], grouped[:, 2:]], axis=2
    )
    band_rows = jnp.arange(3 * LANES, dtype=jnp.int32)[:, None]
    band_cols = jnp.arange(LANES, dtype=jnp.int32)[None, :]
    band_matrix = (jnp.abs(band_rows - band_cols - LANES) <= HALF).astype(jnp.float32)
    running = jnp.einsum(
        "snu,uv->snv", windows, band_matrix, precision=lax.Precision.HIGHEST
    ).reshape(row_count, freq_count)
    denominator = running / (2 * HALF + 1) + 1e-05
    return (real_part / denominator).astype(jnp.bfloat16), (imag_part / denominator).astype(
        jnp.bfloat16
    )


def correlate_kernel(count, index_ref, used_ref, *refs):
    blocks = refs[:count]
    basis_ref, out_ref, table, cross, sems = refs[count:]
    block_rows = blocks[0].shape[0]
    slot_count = out_ref.shape[0]
    columns = used_ref.shape[0]
    slots = slot_count // columns
    copies = [
        pltpu.make_async_copy(
            blocks[k], table.at[pl.ds(k * block_rows, block_rows)], sems.at[k]
        )
        for k in range(count)
    ]
    for copy in copies:
        copy.start()
    zero_rows = table.shape[0] - count * block_rows
    table[pl.ds(count * block_rows, zero_rows)] = jnp.zeros((zero_rows, 8, LANES), table.dtype)

    def clear(i, carry):
        cross[pl.ds(pl.multiple_of(i * 256, 256), 256), :] = jnp.zeros((256, LANES), jnp.float32)
        return carry

    lax.fori_loop(0, slot_count * 8 // 256, clear, 0)
    for copy in copies:
        copy.wait()
    low = lax.broadcasted_iota(jnp.int32, (8, LANES), 0) < 4
    group = 8

    def one_column(column, carry):
        def one_group(g, inner):
            for u in range(group):
                p = column * slots + g * group + u
                a = table[index_ref[0, p]].astype(jnp.float32)
                b = table[index_ref[1, p]].astype(jnp.float32)
                straight = a * b
                crossed = a * pltpu.roll(b, 4, 0)
                real_cross = straight + pltpu.roll(straight, 4, 0)
                imag_cross = crossed - pltpu.roll(crossed, 4, 0)
                start = pl.multiple_of(p * 8, 8)
                cross[pl.ds(start, 8), :] = jnp.where(low, real_cross, imag_cross)
            return inner

        lax.fori_loop(0, (used_ref[column] + group - 1) // group, one_group, 0)
        return carry

    lax.fori_loop(0, columns, one_column, 0)
    step = 256

    def one_dot(i, carry):
        start = pl.multiple_of(i * step * 8, step * 8)
        rows = jnp.concatenate(
            [
                cross[pl.ds(start + k, step, stride=8), :].astype(jnp.bfloat16)
                for k in range(8)
            ],
            axis=1,
        )
        product = jnp.dot(rows, basis_ref[...], preferred_element_type=jnp.float32)
        out_ref[pl.ds(pl.multiple_of(i * step, step), step), :] = product.astype(out_ref.dtype)
        return carry

    lax.fori_loop(0, slot_count // step, one_dot, 0)


def correlate(index, used, blocks, basis):
    count = len(blocks)
    block_rows = blocks[0].shape[0]
    slot_count = index.shape[1]
    vmem = pl.BlockSpec(memory_space=pltpu.VMEM)
    smem = pl.BlockSpec(memory_space=pltpu.SMEM)
    return pl.pallas_call(
        functools.partial(correlate_kernel, count),
        out_shape=jax.ShapeDtypeStruct((slot_count, LAGS), jnp.bfloat16),
        in_specs=[smem, smem] + [pl.BlockSpec(memory_space=pl.ANY)] * count + [vmem],
        out_specs=vmem,
        scratch_shapes=[
            pltpu.VMEM((count * block_rows + 8, 8, LANES), jnp.bfloat16),
            pltpu.VMEM((slot_count * 8, LANES), jnp.float32),
            pltpu.SemaphoreType.DMA((count,)),
        ],
        compiler_params=pltpu.CompilerParams(vmem_limit_bytes=36 * 1024 * 1024),
    )(index, used, *blocks, basis)


def shifts(size):
    up = [(i, (i + 1) % size) for i in range(size)]
    down = [(i, (i - 1) % size) for i in range(size)]
    return up, down


def near_ring(block, axis, reach):
    up, down = shifts(lax.axis_size(axis))
    below, above = [], []
    from_below = from_above = block
    for _ in range(reach):
        from_below = lax.ppermute(from_below, axis, up)
        from_above = lax.ppermute(from_above, axis, down)
        below.append(from_below)
        above.append(from_above)
    return below[::-1] + [block] + above


def far_ring(near, axis, reach):
    size = lax.axis_size(axis)
    up, down = shifts(size)
    below, above = [], []
    from_below, from_above = near[0], near[-1]
    for step in range(reach + 1, size // 2 + 1):
        from_below = lax.ppermute(from_below, axis, up)
        below.append(from_below)
        if step < size - step:
            from_above = lax.ppermute(from_above, axis, down)
            above.append(from_above)
    return above + below[::-1]


def pick(table, digits_high, digits_low):
    rows, cols = table.shape
    hot = (digits_high[:, None] == jnp.arange(rows, dtype=jnp.int32)[None, :]).astype(jnp.bfloat16)
    digits = jnp.concatenate([table // 64, table % 64], axis=1).astype(jnp.bfloat16)
    found = jnp.dot(hot, digits, preferred_element_type=jnp.float32)
    mask = digits_low[:, None] == jnp.arange(cols, dtype=jnp.int32)[None, :]
    high = jnp.sum(jnp.where(mask, found[:, :cols], 0.0), axis=1)
    low = jnp.sum(jnp.where(mask, found[:, cols:], 0.0), axis=1)
    return (high * 64.0 + low).astype(jnp.int32)


def exchange_and_add(partial, group):
    columns = partial.reshape(group, -1, LAGS)
    shares = lax.all_to_all(columns, ("x", "y", "c"), 0, 0, tiled=True)
    return jnp.sum(shares.astype(jnp.float32), axis=0)


def body(spectra, station_pairs, station_home, block_lists):
    xs, ys, cs, zs = (lax.axis_size(n) for n in ("x", "y", "c", "z"))
    z, x = lax.axis_index("z"), lax.axis_index("x")
    owner = z * xs + x
    day = lax.axis_index("y") * cs + lax.axis_index("c")
    days = ys * cs
    column = x * days + day
    columns = xs * days
    rows = spectra.shape[1]
    freqs = spectra.shape[2] // 2
    share = freqs // xs
    scale = 1.0 / math.sqrt(spectra.shape[0] * days)
    pair_slots = station_pairs.shape[0]
    own = pair_slots // days
    plane_rows = rows * xs
    reach = zs // 4

    ends = jnp.concatenate([station_pairs[:, 0], station_pairs[:, 1]], axis=0)
    storage = pick(station_home.reshape(64, -1), ends // 64, ends % 64)
    source_block = storage // rows
    source_row = storage % rows
    wanted = lax.dynamic_index_in_dim(block_lists, owner, 0, keepdims=False)
    hot = (source_block[:, None] == jnp.arange(wanted.shape[0], dtype=jnp.int32)[None, :]).astype(
        jnp.bfloat16
    )
    candidates = jnp.dot(hot, wanted.astype(jnp.bfloat16), preferred_element_type=jnp.float32)
    listed = jnp.any(candidates == source_row.astype(jnp.float32)[:, None], axis=1)
    code = jnp.where(listed, storage, -1).reshape(1, 2 * pair_slots // LANES, LANES)
    code = jnp.broadcast_to(code, (zs * xs,) + code.shape[1:])

    real_part, imag_part = whiten(spectra[0])
    outbound = jnp.concatenate(
        [
            real_part.reshape(rows, xs, share // LANES, LANES),
            imag_part.reshape(rows, xs, share // LANES, LANES),
        ],
        axis=2,
    ).transpose(1, 0, 2, 3)
    block = lax.all_to_all(outbound, "x", 0, 0, tiled=True).reshape(plane_rows, 8, LANES)
    block, code = lax.optimization_barrier((block, code))
    codes = lax.all_to_all(code, ("z", "x"), 0, 0, tiled=True)
    near = near_ring(block, "z", reach)
    codes, _, _ = lax.optimization_barrier((codes, near[reach - 2], near[reach + 2]))
    basis = basis_slice(x * share, share, freqs)

    codes = codes.reshape(zs, xs, 2, days, own).transpose(2, 1, 3, 0, 4)
    first, second = codes.reshape(2, columns, zs * own)
    valid = (first >= 0) & (second >= 0)
    first_plane, second_plane = first // plane_rows, second // plane_rows
    apart = jnp.mod(second_plane - first_plane, zs)
    middle = jnp.where(
        apart <= zs // 2,
        first_plane + apart // 2,
        second_plane + (zs - apart) // 2,
    )
    middle = jnp.where(valid, jnp.mod(middle, zs), -1)

    planes = jnp.arange(zs, dtype=jnp.int32)
    middle_by_owner = middle.reshape(columns, zs, own)
    meets = jnp.sum(
        (middle_by_owner[None] == planes[:, None, None, None]).astype(jnp.float32), axis=3
    )
    slots, returned = 2 * own, own // 2
    crowded = (jnp.max(jnp.sum(meets, axis=2)) > slots) | (jnp.max(meets) > returned)

    here = middle == z
    order = jnp.arange(zs * own, dtype=jnp.int32)
    earlier = (order[:, None] < order[None, :]).astype(jnp.bfloat16)
    rank = jnp.dot(here.astype(jnp.bfloat16), earlier, preferred_element_type=jnp.float32)
    rank = jnp.where(here, rank.astype(jnp.int32), -1)
    first_at = jnp.mod(first_plane - z + reach, zs) * plane_rows + first % plane_rows
    second_at = jnp.mod(second_plane - z + reach, zs) * plane_rows + second % plane_rows
    packed = first_at * 4096 + second_at
    slot_ids = jnp.arange(slots, dtype=jnp.int32)
    taken = rank[:, None, :] == slot_ids[None, :, None]
    chosen = jnp.sum(jnp.where(taken, packed[:, None, :], 0), axis=2).reshape(-1)
    index = jnp.stack([chosen // 4096, chosen % 4096])
    used = jnp.sum(here.astype(jnp.int32), axis=1)

    mine = lax.dynamic_index_in_dim(meets, column, 1, keepdims=False)
    sent = lax.dynamic_index_in_dim(mine, z, 0, keepdims=False)
    begin = jnp.sum(jnp.where(planes[None, :] < planes[:, None], sent[None, :], 0.0), axis=1)
    places = begin.astype(jnp.int32)[:, None] + jnp.arange(returned, dtype=jnp.int32)[None, :]
    send = (places.reshape(-1)[:, None] == slot_ids[None, :]).astype(jnp.bfloat16)
    own_column = lax.dynamic_index_in_dim(middle_by_owner, column, 0, keepdims=False)
    own_middle = lax.dynamic_index_in_dim(own_column, z, 0, keepdims=False)
    ids = jnp.arange(own, dtype=jnp.int32)
    before = (own_middle[:, None] == own_middle[None, :]) & (ids[None, :] < ids[:, None])
    own_at = own_middle * returned + jnp.sum(before.astype(jnp.int32), axis=1)
    own_at = jnp.where(own_middle >= 0, own_at, -1)
    take = (own_at[:, None] == jnp.arange(zs * returned, dtype=jnp.int32)[None, :]).astype(
        jnp.bfloat16
    )

    plane_first = lax.dynamic_slice_in_dim(first, z * own, own, 1).reshape(-1)
    plane_second = lax.dynamic_slice_in_dim(second, z * own, own, 1).reshape(-1)
    plane_codes = jnp.stack([plane_first, plane_second])
    plane_at = jnp.mod(plane_codes // plane_rows - z + reach, zs) * plane_rows
    plane_at = plane_at + jnp.mod(plane_codes, plane_rows)
    plane_index = jnp.where(plane_codes >= 0, plane_at, zs * plane_rows)

    def by_middle(near):
        added = exchange_and_add(correlate(index, used, near, basis), columns)
        leaving = jnp.dot(send, added.astype(jnp.bfloat16), preferred_element_type=jnp.bfloat16)
        arrived = lax.all_to_all(
            leaving.reshape(zs, returned, LAGS), "z", 0, 0, tiled=True
        ).reshape(zs * returned, LAGS)
        return jnp.dot(take, arrived, preferred_element_type=jnp.float32) * scale

    def by_owner(near):
        blocks = near + far_ring(near, "z", reach)
        every = jnp.full((columns,), own, jnp.int32)
        return exchange_and_add(correlate(plane_index, every, blocks, basis), columns) * scale

    return lax.cond(crowded, by_owner, by_middle, near)


def solution(mesh):
    inner = Mesh(mesh.devices.reshape(16, 4, 4, 2), ("z", "x", "y", "c"))
    in_specs = (P(("y", "c"), ("z", "x"), None), P(("z", "x"), None), P(), P())
    out_specs = P(("z", "x", "y", "c"), None)
    return jax.shard_map(
        body, mesh=inner, in_specs=in_specs, out_specs=out_specs, check_vma=False
    )
```

```python
import functools
import math

import jax
import jax.numpy as jnp
from jax import lax
from jax.experimental import pallas as pl
from jax.experimental.pallas import tpu as pltpu
from jax.sharding import Mesh
from jax.sharding import PartitionSpec as P

HALF = 32
LAGS = 256
LANES = 128


def basis_slice(first, count, freqs):
    freq_index = first + jnp.arange(count, dtype=jnp.int32)
    lag_index = jnp.arange(LAGS, dtype=jnp.int32) - LAGS // 2
    phase_steps = jnp.mod(freq_index[:, None] * lag_index[None, :], 2 * freqs)
    angles = phase_steps.astype(jnp.float32) * (2.0 * math.pi / (2 * freqs))
    scaling = 1.0 / math.sqrt(freqs)
    return jnp.concatenate([jnp.cos(angles) * scaling, -jnp.sin(angles) * scaling], axis=0).astype(
        jnp.bfloat16
    )


def whiten(station_rows):
    row_count = station_rows.shape[0]
    freq_count = station_rows.shape[1] // 2
    real_part = station_rows[:, :freq_count]
    imag_part = station_rows[:, freq_count:]
    amplitude = jnp.sqrt(real_part * real_part + imag_part * imag_part)
    extended = jnp.concatenate(
        [amplitude[:, freq_count - LANES :], amplitude, amplitude[:, :LANES]], axis=1
    )
    tile_count = freq_count // LANES
    grouped = extended.reshape(row_count, tile_count + 2, LANES)
    windows = jnp.concatenate(
        [grouped[:, :tile_count], grouped[:, 1 : tile_count + 1], grouped[:, 2:]], axis=2
    )
    band_rows = jnp.arange(3 * LANES, dtype=jnp.int32)[:, None]
    band_cols = jnp.arange(LANES, dtype=jnp.int32)[None, :]
    band_matrix = (jnp.abs(band_rows - band_cols - LANES) <= HALF).astype(jnp.float32)
    running = jnp.einsum(
        "snu,uv->snv", windows, band_matrix, precision=lax.Precision.HIGHEST
    ).reshape(row_count, freq_count)
    denominator = running / (2 * HALF + 1) + 1e-05
    return (real_part / denominator).astype(jnp.bfloat16), (imag_part / denominator).astype(
        jnp.bfloat16
    )


def correlate_kernel(count, index_ref, used_ref, *refs):
    blocks = refs[:count]
    basis_ref, out_ref, table, cross, sems = refs[count:]
    block_rows = blocks[0].shape[0]
    slot_count = out_ref.shape[0]
    columns = used_ref.shape[0]
    slots = slot_count // columns
    copies = [
        pltpu.make_async_copy(
            blocks[k], table.at[pl.ds(k * block_rows, block_rows)], sems.at[k]
        )
        for k in range(count)
    ]
    for copy in copies:
        copy.start()
    zero_rows = table.shape[0] - count * block_rows
    table[pl.ds(count * block_rows, zero_rows)] = jnp.zeros((zero_rows, 8, LANES), table.dtype)

    def clear(i, carry):
        cross[pl.ds(pl.multiple_of(i * 256, 256), 256), :] = jnp.zeros((256, LANES), jnp.float32)
        return carry

    lax.fori_loop(0, slot_count * 8 // 256, clear, 0)
    for copy in copies:
        copy.wait()
    low = lax.broadcasted_iota(jnp.int32, (8, LANES), 0) < 4
    group = 8

    def one_column(column, carry):
        def one_group(g, inner):
            for u in range(group):
                p = column * slots + g * group + u
                a = table[index_ref[0, p]].astype(jnp.float32)
                b = table[index_ref[1, p]].astype(jnp.float32)
                straight = a * b
                crossed = a * pltpu.roll(b, 4, 0)
                real_cross = straight + pltpu.roll(straight, 4, 0)
                imag_cross = crossed - pltpu.roll(crossed, 4, 0)
                start = pl.multiple_of(p * 8, 8)
                cross[pl.ds(start, 8), :] = jnp.where(low, real_cross, imag_cross)
            return inner

        lax.fori_loop(0, (used_ref[column] + group - 1) // group, one_group, 0)
        return carry

    lax.fori_loop(0, columns, one_column, 0)
    step = 256

    def one_dot(i, carry):
        start = pl.multiple_of(i * step * 8, step * 8)
        rows = jnp.concatenate(
            [
                cross[pl.ds(start + k, step, stride=8), :].astype(jnp.bfloat16)
                for k in range(8)
            ],
            axis=1,
        )
        product = jnp.dot(rows, basis_ref[...], preferred_element_type=jnp.float32)
        out_ref[pl.ds(pl.multiple_of(i * step, step), step), :] = product.astype(out_ref.dtype)
        return carry

    lax.fori_loop(0, slot_count // step, one_dot, 0)


def correlate(index, used, blocks, basis):
    count = len(blocks)
    block_rows = blocks[0].shape[0]
    slot_count = index.shape[1]
    vmem = pl.BlockSpec(memory_space=pltpu.VMEM)
    smem = pl.BlockSpec(memory_space=pltpu.SMEM)
    return pl.pallas_call(
        functools.partial(correlate_kernel, count),
        out_shape=jax.ShapeDtypeStruct((slot_count, LAGS), jnp.bfloat16),
        in_specs=[smem, smem] + [pl.BlockSpec(memory_space=pl.ANY)] * count + [vmem],
        out_specs=vmem,
        scratch_shapes=[
            pltpu.VMEM((count * block_rows + 8, 8, LANES), jnp.bfloat16),
            pltpu.VMEM((slot_count * 8, LANES), jnp.float32),
            pltpu.SemaphoreType.DMA((count,)),
        ],
        compiler_params=pltpu.CompilerParams(vmem_limit_bytes=36 * 1024 * 1024),
    )(index, used, *blocks, basis)


def shifts(size):
    up = [(i, (i + 1) % size) for i in range(size)]
    down = [(i, (i - 1) % size) for i in range(size)]
    return up, down


def near_ring(block, axis, reach, codes, basis):
    up, down = shifts(lax.axis_size(axis))
    below, above = [], []
    from_below = from_above = block
    for step in range(reach):
        if step == 2:
            from_below, from_above, codes, basis = lax.optimization_barrier(
                (from_below, from_above, codes, basis)
            )
        from_below = lax.ppermute(from_below, axis, up)
        from_above = lax.ppermute(from_above, axis, down)
        below.append(from_below)
        above.append(from_above)
    return below[::-1] + [block] + above, codes, basis


def far_ring(near, axis, reach):
    size = lax.axis_size(axis)
    up, down = shifts(size)
    below, above = [], []
    from_below, from_above = near[0], near[-1]
    for step in range(reach + 1, size // 2 + 1):
        from_below = lax.ppermute(from_below, axis, up)
        below.append(from_below)
        if step < size - step:
            from_above = lax.ppermute(from_above, axis, down)
            above.append(from_above)
    return above + below[::-1]


def pick(table, digits_high, digits_low):
    rows, cols = table.shape
    hot = (digits_high[:, None] == jnp.arange(rows, dtype=jnp.int32)[None, :]).astype(jnp.bfloat16)
    digits = jnp.concatenate([table // 64, table % 64], axis=1).astype(jnp.bfloat16)
    found = jnp.dot(hot, digits, preferred_element_type=jnp.float32)
    mask = digits_low[:, None] == jnp.arange(cols, dtype=jnp.int32)[None, :]
    high = jnp.sum(jnp.where(mask, found[:, :cols], 0.0), axis=1)
    low = jnp.sum(jnp.where(mask, found[:, cols:], 0.0), axis=1)
    return (high * 64.0 + low).astype(jnp.int32)


def exchange_and_add(partial, group):
    columns = partial.reshape(group, -1, LAGS)
    shares = lax.all_to_all(columns, ("x", "y", "c"), 0, 0, tiled=True)
    return jnp.sum(shares.astype(jnp.float32), axis=0)


def body(spectra, station_pairs, station_home, block_lists):
    xs, ys, cs, zs = (lax.axis_size(n) for n in ("x", "y", "c", "z"))
    z, x = lax.axis_index("z"), lax.axis_index("x")
    owner = z * xs + x
    day = lax.axis_index("y") * cs + lax.axis_index("c")
    days = ys * cs
    column = x * days + day
    columns = xs * days
    rows = spectra.shape[1]
    freqs = spectra.shape[2] // 2
    share = freqs // xs
    scale = 1.0 / math.sqrt(spectra.shape[0] * days)
    pair_slots = station_pairs.shape[0]
    own = pair_slots // days
    plane_rows = rows * xs
    reach = zs // 4

    ends = jnp.concatenate([station_pairs[:, 0], station_pairs[:, 1]], axis=0)
    storage = pick(station_home.reshape(64, -1), ends // 64, ends % 64)
    source_block = storage // rows
    source_row = storage % rows
    wanted = lax.dynamic_index_in_dim(block_lists, owner, 0, keepdims=False)
    hot = (source_block[:, None] == jnp.arange(wanted.shape[0], dtype=jnp.int32)[None, :]).astype(
        jnp.bfloat16
    )
    candidates = jnp.dot(hot, wanted.astype(jnp.bfloat16), preferred_element_type=jnp.float32)
    listed = jnp.any(candidates == source_row.astype(jnp.float32)[:, None], axis=1)
    code = jnp.where(listed, storage, -1).reshape(1, 2 * pair_slots // LANES, LANES)
    code = jnp.broadcast_to(code, (zs * xs,) + code.shape[1:])

    real_part, imag_part = whiten(spectra[0])
    outbound = jnp.concatenate(
        [
            real_part.reshape(rows, xs, share // LANES, LANES),
            imag_part.reshape(rows, xs, share // LANES, LANES),
        ],
        axis=2,
    ).transpose(1, 0, 2, 3)
    block = lax.all_to_all(outbound, "x", 0, 0, tiled=True).reshape(plane_rows, 8, LANES)
    block, code = lax.optimization_barrier((block, code))
    codes = lax.all_to_all(code, ("z", "x"), 0, 0, tiled=True)
    basis = basis_slice(x * share, share, freqs)
    near, codes, basis = near_ring(block, "z", reach, codes, basis)

    planes = jnp.arange(zs, dtype=jnp.int32)
    slots, returned = 2 * own, own // 2
    slot_ids = jnp.arange(slots, dtype=jnp.int32)

    def bookkeeping(codes):
        codes = codes.reshape(zs, xs, 2, days, own).transpose(2, 1, 3, 0, 4)
        first, second = codes.reshape(2, columns, zs * own)
        valid = (first >= 0) & (second >= 0)
        first_plane, second_plane = first // plane_rows, second // plane_rows
        apart = jnp.mod(second_plane - first_plane, zs)
        middle = jnp.where(
            apart <= zs // 2,
            first_plane + apart // 2,
            second_plane + (zs - apart) // 2,
        )
        middle = jnp.where(valid, jnp.mod(middle, zs), -1)

        here = middle == z
        order = jnp.arange(zs * own, dtype=jnp.int32)
        earlier = (order[:, None] < order[None, :]).astype(jnp.bfloat16)
        rank = jnp.dot(here.astype(jnp.bfloat16), earlier, preferred_element_type=jnp.float32)
        rank = jnp.where(here, rank.astype(jnp.int32), -1)
        first_at = jnp.mod(first_plane - z + reach, zs) * plane_rows + first % plane_rows
        second_at = jnp.mod(second_plane - z + reach, zs) * plane_rows + second % plane_rows
        packed = first_at * 4096 + second_at
        taken = rank[:, None, :] == slot_ids[None, :, None]
        chosen = jnp.sum(jnp.where(taken, packed[:, None, :], 0), axis=2).reshape(-1)
        index = jnp.stack([chosen // 4096, chosen % 4096])
        used = jnp.minimum(jnp.sum(here.astype(jnp.int32), axis=1), slots)
        return index, used, middle

    def nothing(codes):
        return (
            jnp.zeros((2, columns * slots), jnp.int32),
            jnp.zeros((columns,), jnp.int32),
            jnp.full((columns, zs * own), -1, jnp.int32),
        )

    index, used, middle = lax.cond(codes[0, 0, 0] >= -1, bookkeeping, nothing, codes)
    partial = correlate(index, used, near, basis)
    added = exchange_and_add(partial, columns)

    middle_by_owner = middle.reshape(columns, zs, own)
    meets = jnp.sum(
        (middle_by_owner[None] == planes[:, None, None, None]).astype(jnp.float32), axis=3
    )
    crowded = (jnp.max(jnp.sum(meets, axis=2)) > slots) | (jnp.max(meets) > returned)

    mine = lax.dynamic_index_in_dim(meets, column, 1, keepdims=False)
    sent = lax.dynamic_index_in_dim(mine, z, 0, keepdims=False)
    begin = jnp.sum(jnp.where(planes[None, :] < planes[:, None], sent[None, :], 0.0), axis=1)
    places = begin.astype(jnp.int32)[:, None] + jnp.arange(returned, dtype=jnp.int32)[None, :]
    send = (places.reshape(-1)[:, None] == slot_ids[None, :]).astype(jnp.bfloat16)
    own_column = lax.dynamic_index_in_dim(middle_by_owner, column, 0, keepdims=False)
    own_middle = lax.dynamic_index_in_dim(own_column, z, 0, keepdims=False)
    ids = jnp.arange(own, dtype=jnp.int32)
    before = (own_middle[:, None] == own_middle[None, :]) & (ids[None, :] < ids[:, None])
    own_at = own_middle * returned + jnp.sum(before.astype(jnp.int32), axis=1)
    own_at = jnp.where(own_middle >= 0, own_at, -1)
    take = (own_at[:, None] == jnp.arange(zs * returned, dtype=jnp.int32)[None, :]).astype(
        jnp.bfloat16
    )
    leaving = jnp.dot(send, added.astype(jnp.bfloat16), preferred_element_type=jnp.bfloat16)
    arrived = lax.all_to_all(
        leaving.reshape(zs, returned, LAGS), "z", 0, 0, tiled=True
    ).reshape(zs * returned, LAGS)
    by_middle = jnp.dot(take, arrived, preferred_element_type=jnp.float32) * scale

    def by_owner(near, codes, by_middle):
        plane = lax.dynamic_slice_in_dim(codes.reshape(zs, xs, 2, pair_slots), z, 1, 0)
        plane_codes = plane[0].transpose(1, 0, 2).reshape(2, xs * pair_slots)
        plane_at = jnp.mod(plane_codes // plane_rows - z + reach, zs) * plane_rows
        plane_at = plane_at + jnp.mod(plane_codes, plane_rows)
        plane_index = jnp.where(plane_codes >= 0, plane_at, zs * plane_rows)
        blocks = near + far_ring(near, "z", reach)
        every = jnp.full((columns,), own, jnp.int32)
        return exchange_and_add(correlate(plane_index, every, blocks, basis), columns) * scale

    return lax.cond(
        crowded, by_owner, lambda near, codes, by_middle: by_middle, near, codes, by_middle
    )


def solution(mesh):
    inner = Mesh(mesh.devices.reshape(16, 4, 4, 2), ("z", "x", "y", "c"))
    in_specs = (P(("y", "c"), ("z", "x"), None), P(("z", "x"), None), P(), P())
    out_specs = P(("z", "x", "y", "c"), None)
    return jax.shard_map(
        body, mesh=inner, in_specs=in_specs, out_specs=out_specs, check_vma=False
    )
```

```python
import functools
import math

import jax
import jax.numpy as jnp
from jax import lax
from jax.experimental import pallas as pl
from jax.experimental.pallas import tpu as pltpu
from jax.sharding import Mesh
from jax.sharding import PartitionSpec as P

HALF = 32
LAGS = 256
LANES = 128


def basis_slice(first, count, freqs):
    freq_index = first + jnp.arange(count, dtype=jnp.int32)
    lag_index = jnp.arange(LAGS, dtype=jnp.int32) - LAGS // 2
    phase_steps = jnp.mod(freq_index[:, None] * lag_index[None, :], 2 * freqs)
    angles = phase_steps.astype(jnp.float32) * (2.0 * math.pi / (2 * freqs))
    scaling = 1.0 / math.sqrt(freqs)
    return jnp.concatenate([jnp.cos(angles) * scaling, -jnp.sin(angles) * scaling], axis=0).astype(
        jnp.bfloat16
    )


def whiten(station_rows):
    row_count = station_rows.shape[0]
    freq_count = station_rows.shape[1] // 2
    real_part = station_rows[:, :freq_count]
    imag_part = station_rows[:, freq_count:]
    amplitude = jnp.sqrt(real_part * real_part + imag_part * imag_part)
    extended = jnp.concatenate(
        [amplitude[:, freq_count - LANES :], amplitude, amplitude[:, :LANES]], axis=1
    )
    tile_count = freq_count // LANES
    grouped = extended.reshape(row_count, tile_count + 2, LANES)
    windows = jnp.concatenate(
        [grouped[:, :tile_count], grouped[:, 1 : tile_count + 1], grouped[:, 2:]], axis=2
    )
    band_rows = jnp.arange(3 * LANES, dtype=jnp.int32)[:, None]
    band_cols = jnp.arange(LANES, dtype=jnp.int32)[None, :]
    band_matrix = (jnp.abs(band_rows - band_cols - LANES) <= HALF).astype(jnp.float32)
    running = jnp.einsum(
        "snu,uv->snv", windows, band_matrix, precision=lax.Precision.HIGHEST
    ).reshape(row_count, freq_count)
    denominator = running / (2 * HALF + 1) + 1e-05
    return (real_part / denominator).astype(jnp.bfloat16), (imag_part / denominator).astype(
        jnp.bfloat16
    )


def correlate_kernel(count, index_ref, used_ref, *refs):
    blocks = refs[:count]
    basis_ref, out_ref, table, cross, sems = refs[count:]
    block_rows = blocks[0].shape[0]
    slot_count = out_ref.shape[0]
    columns = used_ref.shape[0]
    slots = slot_count // columns
    copies = [
        pltpu.make_async_copy(
            blocks[k], table.at[pl.ds(k * block_rows, block_rows)], sems.at[k]
        )
        for k in range(count)
    ]
    for copy in copies:
        copy.start()
    zero_rows = table.shape[0] - count * block_rows
    table[pl.ds(count * block_rows, zero_rows)] = jnp.zeros((zero_rows, 8, LANES), table.dtype)

    def clear(i, carry):
        cross[pl.ds(pl.multiple_of(i * 256, 256), 256), :] = jnp.zeros((256, LANES), jnp.float32)
        return carry

    lax.fori_loop(0, slot_count * 8 // 256, clear, 0)
    for copy in copies:
        copy.wait()
    low = lax.broadcasted_iota(jnp.int32, (8, LANES), 0) < 4
    group = 8

    def one_column(column, carry):
        def one_group(g, inner):
            for u in range(group):
                p = column * slots + g * group + u
                a = table[index_ref[0, p]].astype(jnp.float32)
                b = table[index_ref[1, p]].astype(jnp.float32)
                straight = a * b
                crossed = a * pltpu.roll(b, 4, 0)
                real_cross = straight + pltpu.roll(straight, 4, 0)
                imag_cross = crossed - pltpu.roll(crossed, 4, 0)
                start = pl.multiple_of(p * 8, 8)
                cross[pl.ds(start, 8), :] = jnp.where(low, real_cross, imag_cross)
            return inner

        lax.fori_loop(0, (used_ref[column] + group - 1) // group, one_group, 0)
        return carry

    lax.fori_loop(0, columns, one_column, 0)
    step = 256

    def one_dot(i, carry):
        start = pl.multiple_of(i * step * 8, step * 8)
        rows = jnp.concatenate(
            [
                cross[pl.ds(start + k, step, stride=8), :].astype(jnp.bfloat16)
                for k in range(8)
            ],
            axis=1,
        )
        product = jnp.dot(rows, basis_ref[...], preferred_element_type=jnp.float32)
        out_ref[pl.ds(pl.multiple_of(i * step, step), step), :] = product.astype(out_ref.dtype)
        return carry

    lax.fori_loop(0, slot_count // step, one_dot, 0)


def correlate(index, used, blocks, basis):
    count = len(blocks)
    block_rows = blocks[0].shape[0]
    slot_count = index.shape[1]
    vmem = pl.BlockSpec(memory_space=pltpu.VMEM)
    smem = pl.BlockSpec(memory_space=pltpu.SMEM)
    return pl.pallas_call(
        functools.partial(correlate_kernel, count),
        out_shape=jax.ShapeDtypeStruct((slot_count, LAGS), jnp.bfloat16),
        in_specs=[smem, smem] + [pl.BlockSpec(memory_space=pl.ANY)] * count + [vmem],
        out_specs=vmem,
        scratch_shapes=[
            pltpu.VMEM((count * block_rows + 8, 8, LANES), jnp.bfloat16),
            pltpu.VMEM((slot_count * 8, LANES), jnp.float32),
            pltpu.SemaphoreType.DMA((count,)),
        ],
        compiler_params=pltpu.CompilerParams(vmem_limit_bytes=36 * 1024 * 1024),
    )(index, used, *blocks, basis)


def shifts(size):
    up = [(i, (i + 1) % size) for i in range(size)]
    down = [(i, (i - 1) % size) for i in range(size)]
    return up, down


def near_ring(block, axis, reach, codes, basis, place):
    up, down = shifts(lax.axis_size(axis))
    below, above = [], []
    from_below = from_above = block
    placed = None
    for step in range(reach):
        if step == reach - 2:
            from_below, from_above, codes, basis = lax.optimization_barrier(
                (from_below, from_above, codes, basis)
            )
        if step == reach - 1:
            from_below, from_above, placed = lax.optimization_barrier(
                (from_below, from_above, place(codes))
            )
        from_below = lax.ppermute(from_below, axis, up)
        from_above = lax.ppermute(from_above, axis, down)
        below.append(from_below)
        above.append(from_above)
    return below[::-1] + [block] + above, codes, basis, placed


def place_pairs(codes, zs, xs, days, own, plane_rows, z):
    columns = xs * days
    reach = zs // 4
    codes = codes.reshape(zs, xs, 2, days, own).transpose(2, 1, 3, 0, 4)
    first, second = codes.reshape(2, columns, zs * own)
    valid = (first >= 0) & (second >= 0)
    first_plane, second_plane = first // plane_rows, second // plane_rows
    apart = jnp.mod(second_plane - first_plane, zs)
    middle = jnp.where(
        apart <= zs // 2,
        first_plane + apart // 2,
        second_plane + (zs - apart) // 2,
    )
    middle = jnp.where(valid, jnp.mod(middle, zs), -1)
    loose = jnp.minimum(apart, zs - apart) <= 2 * reach - 2

    planes = jnp.arange(zs, dtype=jnp.int32)
    at = middle[None] == planes[:, None, None]
    load = jnp.sum(at.astype(jnp.float32), axis=2)
    total = jnp.sum(load, axis=0, keepdims=True)
    upto = (planes[None, :] <= planes[:, None]).astype(jnp.float32)
    excess = jnp.sum(upto[:, :, None] * (load * zs - total)[None], axis=1)
    centre = (jnp.max(excess, axis=0) + jnp.min(excess, axis=0)) * 0.5
    flow = jnp.floor((excess - centre) / zs + 0.5)
    rising = jnp.maximum(flow, 0.0)[:, :, None]
    falling = jnp.maximum(-jnp.roll(flow, 1, axis=0), 0.0)[:, :, None]

    movable = (at & loose[None]).astype(jnp.bfloat16)
    order = jnp.arange(zs * own, dtype=jnp.int32)
    earlier = (order[:, None] < order[None, :]).astype(jnp.bfloat16)
    rank = jnp.dot(
        movable.reshape(zs * columns, zs * own), earlier, preferred_element_type=jnp.float32
    ).reshape(zs, columns, zs * own)
    step = jnp.where(rank < rising, 1.0, jnp.where(rank < rising + falling, -1.0, 0.0))
    shift = jnp.sum(movable.astype(jnp.float32) * step, axis=0).astype(jnp.int32)
    middle = jnp.where(valid, jnp.mod(middle + shift, zs), -1)

    first_at = jnp.mod(first_plane - z + reach, zs) * plane_rows + jnp.mod(first, plane_rows)
    second_at = jnp.mod(second_plane - z + reach, zs) * plane_rows + jnp.mod(second, plane_rows)
    return middle, first_at * 4096 + second_at


def fill_slots(middle, packed, slots, z):
    here = middle == z
    order = jnp.arange(middle.shape[1], dtype=jnp.int32)
    earlier = (order[:, None] < order[None, :]).astype(jnp.bfloat16)
    rank = jnp.dot(here.astype(jnp.bfloat16), earlier, preferred_element_type=jnp.float32)
    rank = jnp.where(here, rank.astype(jnp.int32), -1)
    slot_ids = jnp.arange(slots, dtype=jnp.int32)
    taken = rank[:, None, :] == slot_ids[None, :, None]
    chosen = jnp.sum(jnp.where(taken, packed[:, None, :], 0), axis=2).reshape(-1)
    index = jnp.stack([chosen // 4096, chosen % 4096])
    used = jnp.minimum(jnp.sum(here.astype(jnp.int32), axis=1), slots)
    return index, used


def far_ring(near, axis, reach):
    size = lax.axis_size(axis)
    up, down = shifts(size)
    below, above = [], []
    from_below, from_above = near[0], near[-1]
    for step in range(reach + 1, size // 2 + 1):
        from_below = lax.ppermute(from_below, axis, up)
        below.append(from_below)
        if step < size - step:
            from_above = lax.ppermute(from_above, axis, down)
            above.append(from_above)
    return above + below[::-1]


def pick(table, digits_high, digits_low):
    rows, cols = table.shape
    hot = (digits_high[:, None] == jnp.arange(rows, dtype=jnp.int32)[None, :]).astype(jnp.bfloat16)
    digits = jnp.concatenate([table // 64, table % 64], axis=1).astype(jnp.bfloat16)
    found = jnp.dot(hot, digits, preferred_element_type=jnp.float32)
    mask = digits_low[:, None] == jnp.arange(cols, dtype=jnp.int32)[None, :]
    high = jnp.sum(jnp.where(mask, found[:, :cols], 0.0), axis=1)
    low = jnp.sum(jnp.where(mask, found[:, cols:], 0.0), axis=1)
    return (high * 64.0 + low).astype(jnp.int32)


def exchange_and_add(partial, group):
    columns = partial.reshape(group, -1, LAGS)
    shares = lax.all_to_all(columns, ("x", "y", "c"), 0, 0, tiled=True)
    return jnp.sum(shares.astype(jnp.float32), axis=0)


def body(spectra, station_pairs, station_home, block_lists):
    xs, ys, cs, zs = (lax.axis_size(n) for n in ("x", "y", "c", "z"))
    z, x = lax.axis_index("z"), lax.axis_index("x")
    owner = z * xs + x
    day = lax.axis_index("y") * cs + lax.axis_index("c")
    days = ys * cs
    column = x * days + day
    columns = xs * days
    rows = spectra.shape[1]
    freqs = spectra.shape[2] // 2
    share = freqs // xs
    scale = 1.0 / math.sqrt(spectra.shape[0] * days)
    pair_slots = station_pairs.shape[0]
    own = pair_slots // days
    plane_rows = rows * xs
    reach = zs // 4

    ends = jnp.concatenate([station_pairs[:, 0], station_pairs[:, 1]], axis=0)
    storage = pick(station_home.reshape(64, -1), ends // 64, ends % 64)
    source_block = storage // rows
    source_row = storage % rows
    wanted = lax.dynamic_index_in_dim(block_lists, owner, 0, keepdims=False)
    hot = (source_block[:, None] == jnp.arange(wanted.shape[0], dtype=jnp.int32)[None, :]).astype(
        jnp.bfloat16
    )
    candidates = jnp.dot(hot, wanted.astype(jnp.bfloat16), preferred_element_type=jnp.float32)
    listed = jnp.any(candidates == source_row.astype(jnp.float32)[:, None], axis=1)
    code = jnp.where(listed, storage, -1).reshape(1, 2 * pair_slots // LANES, LANES)
    code = jnp.broadcast_to(code, (zs * xs,) + code.shape[1:])

    real_part, imag_part = whiten(spectra[0])
    outbound = jnp.concatenate(
        [
            real_part.reshape(rows, xs, share // LANES, LANES),
            imag_part.reshape(rows, xs, share // LANES, LANES),
        ],
        axis=2,
    ).transpose(1, 0, 2, 3)
    block = lax.all_to_all(outbound, "x", 0, 0, tiled=True).reshape(plane_rows, 8, LANES)
    block, code = lax.optimization_barrier((block, code))
    codes = lax.all_to_all(code, ("z", "x"), 0, 0, tiled=True)
    basis = basis_slice(x * share, share, freqs)
    planes = jnp.arange(zs, dtype=jnp.int32)
    slots, returned = own + own // 4, own // 2
    slot_ids = jnp.arange(slots, dtype=jnp.int32)

    def place(codes):
        def first_branch(codes):
            return place_pairs(codes, zs, xs, days, own, plane_rows, z)

        def second_branch(codes):
            none = jnp.full((columns, zs * own), -1, jnp.int32)
            return none, none

        return lax.cond(codes[0, 0, 0] >= -1, first_branch, second_branch, codes)

    near, codes, basis, placed = near_ring(block, "z", reach, codes, basis, place)
    middle, packed = placed

    def first_branch(middle, packed):
        return fill_slots(middle, packed, slots, z)

    def second_branch(middle, packed):
        return jnp.zeros((2, columns * slots), jnp.int32), jnp.zeros((columns,), jnp.int32)

    index, used = lax.cond(codes[0, 0, 0] >= -1, first_branch, second_branch, middle, packed)
    partial = correlate(index, used, near, basis)
    added = exchange_and_add(partial, columns)

    middle_by_owner = middle.reshape(columns, zs, own)
    meets = jnp.sum(
        (middle_by_owner[None] == planes[:, None, None, None]).astype(jnp.float32), axis=3
    )
    crowded = (jnp.max(jnp.sum(meets, axis=2)) > slots) | (jnp.max(meets) > returned)

    mine = lax.dynamic_index_in_dim(meets, column, 1, keepdims=False)
    sent = lax.dynamic_index_in_dim(mine, z, 0, keepdims=False)
    begin = jnp.sum(jnp.where(planes[None, :] < planes[:, None], sent[None, :], 0.0), axis=1)
    places = begin.astype(jnp.int32)[:, None] + jnp.arange(returned, dtype=jnp.int32)[None, :]
    send = (places.reshape(-1)[:, None] == slot_ids[None, :]).astype(jnp.bfloat16)
    own_column = lax.dynamic_index_in_dim(middle_by_owner, column, 0, keepdims=False)
    own_middle = lax.dynamic_index_in_dim(own_column, z, 0, keepdims=False)
    ids = jnp.arange(own, dtype=jnp.int32)
    before = (own_middle[:, None] == own_middle[None, :]) & (ids[None, :] < ids[:, None])
    own_at = own_middle * returned + jnp.sum(before.astype(jnp.int32), axis=1)
    own_at = jnp.where(own_middle >= 0, own_at, -1)
    take = (own_at[:, None] == jnp.arange(zs * returned, dtype=jnp.int32)[None, :]).astype(
        jnp.bfloat16
    )
    leaving = jnp.dot(send, added.astype(jnp.bfloat16), preferred_element_type=jnp.bfloat16)
    arrived = lax.all_to_all(
        leaving.reshape(zs, returned, LAGS), "z", 0, 0, tiled=True
    ).reshape(zs * returned, LAGS)
    by_middle = jnp.dot(take, arrived, preferred_element_type=jnp.float32) * scale

    def by_owner(near, codes, by_middle):
        plane = lax.dynamic_slice_in_dim(codes.reshape(zs, xs, 2, pair_slots), z, 1, 0)
        plane_codes = plane[0].transpose(1, 0, 2).reshape(2, xs * pair_slots)
        plane_at = jnp.mod(plane_codes // plane_rows - z + reach, zs) * plane_rows
        plane_at = plane_at + jnp.mod(plane_codes, plane_rows)
        plane_index = jnp.where(plane_codes >= 0, plane_at, zs * plane_rows)
        blocks = near + far_ring(near, "z", reach)
        every = jnp.full((columns,), own, jnp.int32)
        return exchange_and_add(correlate(plane_index, every, blocks, basis), columns) * scale

    return lax.cond(
        crowded, by_owner, lambda near, codes, by_middle: by_middle, near, codes, by_middle
    )


def solution(mesh):
    inner = Mesh(mesh.devices.reshape(16, 4, 4, 2), ("z", "x", "y", "c"))
    in_specs = (P(("y", "c"), ("z", "x"), None), P(("z", "x"), None), P(), P())
    out_specs = P(("z", "x", "y", "c"), None)
    return jax.shard_map(
        body, mesh=inner, in_specs=in_specs, out_specs=out_specs, check_vma=False
    )
```

```python
import functools
import math

import jax
import jax.numpy as jnp
from jax import lax
from jax.experimental import pallas as pl
from jax.experimental.pallas import tpu as pltpu
from jax.sharding import Mesh
from jax.sharding import PartitionSpec as P

HALF = 32
LAGS = 256
LANES = 128


def basis_slice(first, count, freqs):
    freq_index = first + jnp.arange(count, dtype=jnp.int32)
    lag_index = jnp.arange(LAGS, dtype=jnp.int32) - LAGS // 2
    phase_steps = jnp.mod(freq_index[:, None] * lag_index[None, :], 2 * freqs)
    angles = phase_steps.astype(jnp.float32) * (2.0 * math.pi / (2 * freqs))
    scaling = 1.0 / math.sqrt(freqs)
    return jnp.concatenate([jnp.cos(angles) * scaling, -jnp.sin(angles) * scaling], axis=0).astype(
        jnp.bfloat16
    )


def whiten(station_rows):
    row_count = station_rows.shape[0]
    freq_count = station_rows.shape[1] // 2
    real_part = station_rows[:, :freq_count]
    imag_part = station_rows[:, freq_count:]
    amplitude = jnp.sqrt(real_part * real_part + imag_part * imag_part)
    extended = jnp.concatenate(
        [amplitude[:, freq_count - LANES :], amplitude, amplitude[:, :LANES]], axis=1
    )
    tile_count = freq_count // LANES
    grouped = extended.reshape(row_count, tile_count + 2, LANES)
    windows = jnp.concatenate(
        [grouped[:, :tile_count], grouped[:, 1 : tile_count + 1], grouped[:, 2:]], axis=2
    )
    band_rows = jnp.arange(3 * LANES, dtype=jnp.int32)[:, None]
    band_cols = jnp.arange(LANES, dtype=jnp.int32)[None, :]
    band_matrix = (jnp.abs(band_rows - band_cols - LANES) <= HALF).astype(jnp.float32)
    running = jnp.einsum(
        "snu,uv->snv", windows, band_matrix, precision=lax.Precision.HIGHEST
    ).reshape(row_count, freq_count)
    denominator = running / (2 * HALF + 1) + 1e-05
    return (real_part / denominator).astype(jnp.bfloat16), (imag_part / denominator).astype(
        jnp.bfloat16
    )


def correlate_kernel(count, index_ref, used_ref, *refs):
    blocks = refs[:count]
    basis_ref, out_ref, table, cross, sems = refs[count:]
    block_rows = blocks[0].shape[0]
    slot_count = out_ref.shape[0]
    columns = used_ref.shape[0]
    slots = slot_count // columns
    copies = [
        pltpu.make_async_copy(
            blocks[k], table.at[pl.ds(k * block_rows, block_rows)], sems.at[k]
        )
        for k in range(count)
    ]
    for copy in copies:
        copy.start()
    zero_rows = table.shape[0] - count * block_rows
    table[pl.ds(count * block_rows, zero_rows)] = jnp.zeros((zero_rows, 8, LANES), table.dtype)

    def clear(i, carry):
        cross[pl.ds(pl.multiple_of(i * 256, 256), 256), :] = jnp.zeros((256, LANES), jnp.float32)
        return carry

    lax.fori_loop(0, slot_count * 8 // 256, clear, 0)
    for copy in copies:
        copy.wait()
    low = lax.broadcasted_iota(jnp.int32, (8, LANES), 0) < 4
    group = 8
    whole = slots // 32 * 32

    def one_pair(p):
        a = table[index_ref[0, p]].astype(jnp.float32)
        b = table[index_ref[1, p]].astype(jnp.float32)
        swapped_a = pltpu.roll(a, 4, 0)
        swapped_b = pltpu.roll(b, 4, 0)
        real_b = jnp.where(low, b, swapped_b)
        imag_b = jnp.where(low, swapped_b, -b)
        start = pl.multiple_of(p * 8, 8)
        cross[pl.ds(start, 8), :] = a * real_b + swapped_a * imag_b

    def one_column(column, carry):
        base = column * slots
        for u in range(whole):
            one_pair(base + u)

        def one_group(g, inner):
            for u in range(group):
                one_pair(base + whole + g * group + u)
            return inner

        extra = jnp.maximum(used_ref[column] - whole + group - 1, 0) // group
        lax.fori_loop(0, extra, one_group, 0)
        return carry

    lax.fori_loop(0, columns, one_column, 0)
    step = 256

    def one_dot(i, carry):
        start = pl.multiple_of(i * step * 8, step * 8)
        rows = jnp.concatenate(
            [
                cross[pl.ds(start + k, step, stride=8), :].astype(jnp.bfloat16)
                for k in range(8)
            ],
            axis=1,
        )
        product = jnp.dot(rows, basis_ref[...], preferred_element_type=jnp.float32)
        out_ref[pl.ds(pl.multiple_of(i * step, step), step), :] = product.astype(out_ref.dtype)
        return carry

    lax.fori_loop(0, slot_count // step, one_dot, 0)


def correlate(index, used, blocks, basis):
    count = len(blocks)
    block_rows = blocks[0].shape[0]
    slot_count = index.shape[1]
    vmem = pl.BlockSpec(memory_space=pltpu.VMEM)
    smem = pl.BlockSpec(memory_space=pltpu.SMEM)
    return pl.pallas_call(
        functools.partial(correlate_kernel, count),
        out_shape=jax.ShapeDtypeStruct((slot_count, LAGS), jnp.bfloat16),
        in_specs=[smem, smem] + [pl.BlockSpec(memory_space=pl.ANY)] * count + [vmem],
        out_specs=vmem,
        scratch_shapes=[
            pltpu.VMEM((count * block_rows + 8, 8, LANES), jnp.bfloat16),
            pltpu.VMEM((slot_count * 8, LANES), jnp.float32),
            pltpu.SemaphoreType.DMA((count,)),
        ],
        compiler_params=pltpu.CompilerParams(vmem_limit_bytes=36 * 1024 * 1024),
    )(index, used, *blocks, basis)


def shifts(size):
    up = [(i, (i + 1) % size) for i in range(size)]
    down = [(i, (i - 1) % size) for i in range(size)]
    return up, down


def near_ring(block, axis, reach, codes, basis, place):
    up, down = shifts(lax.axis_size(axis))
    below, above = [], []
    from_below = from_above = block
    placed = None
    for step in range(reach):
        if step == reach - 2:
            from_below, from_above, codes, basis = lax.optimization_barrier(
                (from_below, from_above, codes, basis)
            )
        if step == reach - 1:
            from_below, from_above, placed = lax.optimization_barrier(
                (from_below, from_above, place(codes))
            )
        from_below = lax.ppermute(from_below, axis, up)
        from_above = lax.ppermute(from_above, axis, down)
        below.append(from_below)
        above.append(from_above)
    return below[::-1] + [block] + above, codes, basis, placed


def place_pairs(codes, zs, xs, days, own, plane_rows, z):
    columns = xs * days
    reach = zs // 4
    codes = codes.reshape(zs, xs, 2, days, own).transpose(2, 1, 3, 0, 4)
    first, second = codes.reshape(2, columns, zs * own)
    valid = (first >= 0) & (second >= 0)
    first_plane, second_plane = first // plane_rows, second // plane_rows
    apart = jnp.mod(second_plane - first_plane, zs)
    middle = jnp.where(
        apart <= zs // 2,
        first_plane + apart // 2,
        second_plane + (zs - apart) // 2,
    )
    middle = jnp.where(valid, jnp.mod(middle, zs), -1)
    loose = jnp.minimum(apart, zs - apart) <= 2 * reach - 2

    planes = jnp.arange(zs, dtype=jnp.int32)
    at = middle[None] == planes[:, None, None]
    load = jnp.sum(at.astype(jnp.float32), axis=2)
    total = jnp.sum(load, axis=0, keepdims=True)
    upto = (planes[None, :] <= planes[:, None]).astype(jnp.float32)
    excess = jnp.sum(upto[:, :, None] * (load * zs - total)[None], axis=1)
    centre = (jnp.max(excess, axis=0) + jnp.min(excess, axis=0)) * 0.5
    flow = jnp.floor((excess - centre) / zs + 0.5)
    rising = jnp.maximum(flow, 0.0)[:, :, None]
    falling = jnp.maximum(-jnp.roll(flow, 1, axis=0), 0.0)[:, :, None]

    movable = (at & loose[None]).astype(jnp.bfloat16)
    order = jnp.arange(zs * own, dtype=jnp.int32)
    earlier = (order[:, None] < order[None, :]).astype(jnp.bfloat16)
    rank = jnp.dot(
        movable.reshape(zs * columns, zs * own), earlier, preferred_element_type=jnp.float32
    ).reshape(zs, columns, zs * own)
    step = jnp.where(rank < rising, 1.0, jnp.where(rank < rising + falling, -1.0, 0.0))
    shift = jnp.sum(movable.astype(jnp.float32) * step, axis=0).astype(jnp.int32)
    middle = jnp.where(valid, jnp.mod(middle + shift, zs), -1)

    first_at = jnp.mod(first_plane - z + reach, zs) * plane_rows + jnp.mod(first, plane_rows)
    second_at = jnp.mod(second_plane - z + reach, zs) * plane_rows + jnp.mod(second, plane_rows)
    return middle, first_at * 4096 + second_at


def fill_slots(middle, packed, slots, z):
    here = middle == z
    order = jnp.arange(middle.shape[1], dtype=jnp.int32)
    earlier = (order[:, None] < order[None, :]).astype(jnp.bfloat16)
    rank = jnp.dot(here.astype(jnp.bfloat16), earlier, preferred_element_type=jnp.float32)
    rank = jnp.where(here, rank.astype(jnp.int32), -1)
    slot_ids = jnp.arange(slots, dtype=jnp.int32)
    taken = rank[:, None, :] == slot_ids[None, :, None]
    chosen = jnp.sum(jnp.where(taken, packed[:, None, :], 0), axis=2).reshape(-1)
    index = jnp.stack([chosen // 4096, chosen % 4096])
    used = jnp.minimum(jnp.sum(here.astype(jnp.int32), axis=1), slots)
    return index, used


def far_ring(near, axis, reach):
    size = lax.axis_size(axis)
    up, down = shifts(size)
    below, above = [], []
    from_below, from_above = near[0], near[-1]
    for step in range(reach + 1, size // 2 + 1):
        from_below = lax.ppermute(from_below, axis, up)
        below.append(from_below)
        if step < size - step:
            from_above = lax.ppermute(from_above, axis, down)
            above.append(from_above)
    return above + below[::-1]


def pick(table, digits_high, digits_low):
    rows, cols = table.shape
    hot = (digits_high[:, None] == jnp.arange(rows, dtype=jnp.int32)[None, :]).astype(jnp.bfloat16)
    digits = jnp.concatenate([table // 64, table % 64], axis=1).astype(jnp.bfloat16)
    found = jnp.dot(hot, digits, preferred_element_type=jnp.float32)
    mask = digits_low[:, None] == jnp.arange(cols, dtype=jnp.int32)[None, :]
    high = jnp.sum(jnp.where(mask, found[:, :cols], 0.0), axis=1)
    low = jnp.sum(jnp.where(mask, found[:, cols:], 0.0), axis=1)
    return (high * 64.0 + low).astype(jnp.int32)


def exchange_and_add(partial, group):
    columns = partial.reshape(group, -1, LAGS)
    shares = lax.all_to_all(columns, ("x", "y", "c"), 0, 0, tiled=True)
    return jnp.sum(shares.astype(jnp.float32), axis=0)


def body(spectra, station_pairs, station_home, block_lists):
    xs, ys, cs, zs = (lax.axis_size(n) for n in ("x", "y", "c", "z"))
    z, x = lax.axis_index("z"), lax.axis_index("x")
    owner = z * xs + x
    day = lax.axis_index("y") * cs + lax.axis_index("c")
    days = ys * cs
    column = x * days + day
    columns = xs * days
    rows = spectra.shape[1]
    freqs = spectra.shape[2] // 2
    share = freqs // xs
    scale = 1.0 / math.sqrt(spectra.shape[0] * days)
    pair_slots = station_pairs.shape[0]
    own = pair_slots // days
    plane_rows = rows * xs
    reach = zs // 4

    ends = jnp.concatenate([station_pairs[:, 0], station_pairs[:, 1]], axis=0)
    storage = pick(station_home.reshape(64, -1), ends // 64, ends % 64)
    source_block = storage // rows
    source_row = storage % rows
    wanted = lax.dynamic_index_in_dim(block_lists, owner, 0, keepdims=False)
    hot = (source_block[:, None] == jnp.arange(wanted.shape[0], dtype=jnp.int32)[None, :]).astype(
        jnp.bfloat16
    )
    candidates = jnp.dot(hot, wanted.astype(jnp.bfloat16), preferred_element_type=jnp.float32)
    listed = jnp.any(candidates == source_row.astype(jnp.float32)[:, None], axis=1)
    code = jnp.where(listed, storage, -1).reshape(1, 2 * pair_slots // LANES, LANES)
    code = jnp.broadcast_to(code, (zs * xs,) + code.shape[1:])

    real_part, imag_part = whiten(spectra[0])
    outbound = jnp.concatenate(
        [
            real_part.reshape(rows, xs, share // LANES, LANES),
            imag_part.reshape(rows, xs, share // LANES, LANES),
        ],
        axis=2,
    ).transpose(1, 0, 2, 3)
    block = lax.all_to_all(outbound, "x", 0, 0, tiled=True).reshape(plane_rows, 8, LANES)
    codes = lax.all_to_all(code, ("z", "x"), 0, 0, tiled=True)
    basis = basis_slice(x * share, share, freqs)
    planes = jnp.arange(zs, dtype=jnp.int32)
    slots, returned = own + own // 4, own // 2
    slot_ids = jnp.arange(slots, dtype=jnp.int32)

    def place(codes):
        def first_branch(codes):
            return place_pairs(codes, zs, xs, days, own, plane_rows, z)

        def second_branch(codes):
            none = jnp.full((columns, zs * own), -1, jnp.int32)
            return none, none

        return lax.cond(codes[0, 0, 0] >= -1, first_branch, second_branch, codes)

    near, codes, basis, placed = near_ring(block, "z", reach, codes, basis, place)
    middle, packed = placed

    def first_branch(middle, packed):
        return fill_slots(middle, packed, slots, z)

    def second_branch(middle, packed):
        return jnp.zeros((2, columns * slots), jnp.int32), jnp.zeros((columns,), jnp.int32)

    index, used = lax.cond(codes[0, 0, 0] >= -1, first_branch, second_branch, middle, packed)
    partial = correlate(index, used, near, basis)
    added = exchange_and_add(partial, columns)

    middle_by_owner = middle.reshape(columns, zs, own)
    meets = jnp.sum(
        (middle_by_owner[None] == planes[:, None, None, None]).astype(jnp.float32), axis=3
    )
    crowded = (jnp.max(jnp.sum(meets, axis=2)) > slots) | (jnp.max(meets) > returned)

    mine = lax.dynamic_index_in_dim(meets, column, 1, keepdims=False)
    sent = lax.dynamic_index_in_dim(mine, z, 0, keepdims=False)
    begin = jnp.sum(jnp.where(planes[None, :] < planes[:, None], sent[None, :], 0.0), axis=1)
    places = begin.astype(jnp.int32)[:, None] + jnp.arange(returned, dtype=jnp.int32)[None, :]
    send = (places.reshape(-1)[:, None] == slot_ids[None, :]).astype(jnp.bfloat16)
    own_column = lax.dynamic_index_in_dim(middle_by_owner, column, 0, keepdims=False)
    own_middle = lax.dynamic_index_in_dim(own_column, z, 0, keepdims=False)
    ids = jnp.arange(own, dtype=jnp.int32)
    before = (own_middle[:, None] == own_middle[None, :]) & (ids[None, :] < ids[:, None])
    own_at = own_middle * returned + jnp.sum(before.astype(jnp.int32), axis=1)
    own_at = jnp.where(own_middle >= 0, own_at, -1)
    take = (own_at[:, None] == jnp.arange(zs * returned, dtype=jnp.int32)[None, :]).astype(
        jnp.bfloat16
    )
    leaving = jnp.dot(send, added.astype(jnp.bfloat16), preferred_element_type=jnp.bfloat16)
    arrived = lax.all_to_all(
        leaving.reshape(zs, returned, LAGS), "z", 0, 0, tiled=True
    ).reshape(zs * returned, LAGS)
    by_middle = jnp.dot(take, arrived, preferred_element_type=jnp.float32) * scale

    def by_owner(near, codes, by_middle):
        plane = lax.dynamic_slice_in_dim(codes.reshape(zs, xs, 2, pair_slots), z, 1, 0)
        plane_codes = plane[0].transpose(1, 0, 2).reshape(2, xs * pair_slots)
        plane_at = jnp.mod(plane_codes // plane_rows - z + reach, zs) * plane_rows
        plane_at = plane_at + jnp.mod(plane_codes, plane_rows)
        plane_index = jnp.where(plane_codes >= 0, plane_at, zs * plane_rows)
        blocks = near + far_ring(near, "z", reach)
        every = jnp.full((columns,), own, jnp.int32)
        return exchange_and_add(correlate(plane_index, every, blocks, basis), columns) * scale

    return lax.cond(
        crowded, by_owner, lambda near, codes, by_middle: by_middle, near, codes, by_middle
    )


def solution(mesh):
    inner = Mesh(mesh.devices.reshape(16, 4, 4, 2), ("z", "x", "y", "c"))
    in_specs = (P(("y", "c"), ("z", "x"), None), P(("z", "x"), None), P(), P())
    out_specs = P(("z", "x", "y", "c"), None)
    return jax.shard_map(
        body, mesh=inner, in_specs=in_specs, out_specs=out_specs, check_vma=False
    )
```

```python
import functools
import math

import jax
import jax.numpy as jnp
from jax import lax
from jax.experimental import pallas as pl
from jax.experimental.pallas import tpu as pltpu
from jax.sharding import Mesh
from jax.sharding import PartitionSpec as P

HALF = 32
LAGS = 256
LANES = 128


def basis_slice(first, count, freqs):
    freq_index = first + jnp.arange(count, dtype=jnp.int32)
    lag_index = jnp.arange(LAGS, dtype=jnp.int32) - LAGS // 2
    phase_steps = jnp.mod(freq_index[:, None] * lag_index[None, :], 2 * freqs)
    angles = phase_steps.astype(jnp.float32) * (2.0 * math.pi / (2 * freqs))
    scaling = 1.0 / math.sqrt(freqs)
    return jnp.concatenate([jnp.cos(angles) * scaling, -jnp.sin(angles) * scaling], axis=0).astype(
        jnp.bfloat16
    )


def whiten(station_rows):
    row_count = station_rows.shape[0]
    freq_count = station_rows.shape[1] // 2
    real_part = station_rows[:, :freq_count]
    imag_part = station_rows[:, freq_count:]
    amplitude = jnp.sqrt(real_part * real_part + imag_part * imag_part)
    extended = jnp.concatenate(
        [amplitude[:, freq_count - LANES :], amplitude, amplitude[:, :LANES]], axis=1
    )
    tile_count = freq_count // LANES
    grouped = extended.reshape(row_count, tile_count + 2, LANES)
    windows = jnp.concatenate(
        [grouped[:, :tile_count], grouped[:, 1 : tile_count + 1], grouped[:, 2:]], axis=2
    )
    band_rows = jnp.arange(3 * LANES, dtype=jnp.int32)[:, None]
    band_cols = jnp.arange(LANES, dtype=jnp.int32)[None, :]
    band_matrix = (jnp.abs(band_rows - band_cols - LANES) <= HALF).astype(jnp.float32)
    running = jnp.einsum(
        "snu,uv->snv", windows, band_matrix, precision=lax.Precision.HIGHEST
    ).reshape(row_count, freq_count)
    denominator = running / (2 * HALF + 1) + 1e-05
    return (real_part / denominator).astype(jnp.bfloat16), (imag_part / denominator).astype(
        jnp.bfloat16
    )


def load_table(blocks, table, sems):
    count, block_rows = len(blocks), blocks[0].shape[0]
    copies = [
        pltpu.make_async_copy(
            blocks[k], table.at[pl.ds(k * block_rows, block_rows)], sems.at[k]
        )
        for k in range(count)
    ]
    for copy in copies:
        copy.start()
    zero_rows = table.shape[0] - count * block_rows
    table[pl.ds(count * block_rows, zero_rows)] = jnp.zeros((zero_rows, 8, LANES), table.dtype)
    return copies


def loading_kernel(count, index_ref, used_ref, *refs):
    blocks = refs[:count]
    basis_ref, out_ref, table, cross, sems = refs[count:]
    copies = load_table(blocks, table, sems)
    clear_rows(cross)
    for copy in copies:
        copy.wait()
    cross_and_contract(index_ref, used_ref, table, basis_ref, out_ref, cross)


def reusing_kernel(index_ref, used_ref, table, basis_ref, out_ref, cross):
    clear_rows(cross)
    cross_and_contract(index_ref, used_ref, table, basis_ref, out_ref, cross)


def clear_rows(cross):
    def clear(i, carry):
        cross[pl.ds(pl.multiple_of(i * 256, 256), 256), :] = jnp.zeros((256, LANES), jnp.float32)
        return carry

    lax.fori_loop(0, cross.shape[0] // 256, clear, 0)


def cross_and_contract(index_ref, used_ref, table, basis_ref, out_ref, cross):
    slot_count = out_ref.shape[0]
    columns = used_ref.shape[0]
    slots = slot_count // columns
    low = lax.broadcasted_iota(jnp.int32, (8, LANES), 0) < 4
    group = 8
    whole = slots // 32 * 32

    def one_pair(p):
        a = table[index_ref[0, p]].astype(jnp.float32)
        b = table[index_ref[1, p]].astype(jnp.float32)
        swapped_a = pltpu.roll(a, 4, 0)
        swapped_b = pltpu.roll(b, 4, 0)
        real_b = jnp.where(low, b, swapped_b)
        imag_b = jnp.where(low, swapped_b, -b)
        start = pl.multiple_of(p * 8, 8)
        cross[pl.ds(start, 8), :] = a * real_b + swapped_a * imag_b

    def one_column(column, carry):
        base = column * slots
        for u in range(whole):
            one_pair(base + u)

        def one_group(g, inner):
            for u in range(group):
                one_pair(base + whole + g * group + u)
            return inner

        extra = jnp.maximum(used_ref[column] - whole + group - 1, 0) // group
        lax.fori_loop(0, extra, one_group, 0)
        return carry

    lax.fori_loop(0, columns, one_column, 0)
    step = 128

    def one_dot(i, carry):
        start = pl.multiple_of(i * step * 8, step * 8)
        rows = jnp.concatenate(
            [
                cross[pl.ds(start + k, step, stride=8), :].astype(jnp.bfloat16)
                for k in range(8)
            ],
            axis=1,
        )
        product = jnp.dot(rows, basis_ref[...], preferred_element_type=jnp.float32)
        out_ref[pl.ds(pl.multiple_of(i * step, step), step), :] = product.astype(out_ref.dtype)
        return carry

    lax.fori_loop(0, slot_count // step, one_dot, 0)


def correlate(index, used, blocks, basis):
    count = len(blocks)
    block_rows = blocks[0].shape[0]
    slot_count = index.shape[1]
    vmem = pl.BlockSpec(memory_space=pltpu.VMEM)
    smem = pl.BlockSpec(memory_space=pltpu.SMEM)
    return pl.pallas_call(
        functools.partial(loading_kernel, count),
        out_shape=[
            jax.ShapeDtypeStruct((slot_count, LAGS), jnp.bfloat16),
            jax.ShapeDtypeStruct((count * block_rows + 8, 8, LANES), jnp.bfloat16),
        ],
        in_specs=[smem, smem] + [pl.BlockSpec(memory_space=pl.ANY)] * count + [vmem],
        out_specs=[vmem, vmem],
        scratch_shapes=[
            pltpu.VMEM((slot_count * 8, LANES), jnp.float32),
            pltpu.SemaphoreType.DMA((count,)),
        ],
        compiler_params=pltpu.CompilerParams(vmem_limit_bytes=40 * 1024 * 1024),
    )(index, used, *blocks, basis)


def correlate_again(index, used, table, basis):
    slot_count = index.shape[1]
    vmem = pl.BlockSpec(memory_space=pltpu.VMEM)
    smem = pl.BlockSpec(memory_space=pltpu.SMEM)
    return pl.pallas_call(
        reusing_kernel,
        out_shape=jax.ShapeDtypeStruct((slot_count, LAGS), jnp.bfloat16),
        in_specs=[smem, smem, vmem, vmem],
        out_specs=vmem,
        scratch_shapes=[pltpu.VMEM((slot_count * 8, LANES), jnp.float32)],
        compiler_params=pltpu.CompilerParams(vmem_limit_bytes=32 * 1024 * 1024),
        cost_estimate=pl.CostEstimate(
            flops=2 * slot_count * 8 * LANES * LAGS, bytes_accessed=8 << 20, transcendentals=0
        ),
    )(index, used, table, basis)


def shifts(size):
    up = [(i, (i + 1) % size) for i in range(size)]
    down = [(i, (i - 1) % size) for i in range(size)]
    return up, down


def near_ring(block, axis, reach, codes, basis, place):
    up, down = shifts(lax.axis_size(axis))
    below, above = [], []
    from_below = from_above = block
    placed = None
    for step in range(reach):
        if step == reach - 2:
            from_below, from_above, codes, basis = lax.optimization_barrier(
                (from_below, from_above, codes, basis)
            )
        if step == reach - 1:
            from_below, from_above, placed = lax.optimization_barrier(
                (from_below, from_above, place(codes))
            )
        from_below = lax.ppermute(from_below, axis, up)
        from_above = lax.ppermute(from_above, axis, down)
        below.append(from_below)
        above.append(from_above)
    return below[::-1] + [block] + above, codes, basis, placed


def place_pairs(codes, zs, xs, days, own, plane_rows, z):
    columns = xs * days
    reach = zs // 4
    codes = codes.reshape(zs, xs, 2, days, own).transpose(2, 1, 3, 0, 4)
    first, second = codes.reshape(2, columns, zs * own)
    valid = (first >= 0) & (second >= 0)
    first_plane, second_plane = first // plane_rows, second // plane_rows
    apart = jnp.mod(second_plane - first_plane, zs)
    middle = jnp.where(
        apart <= zs // 2,
        first_plane + apart // 2,
        second_plane + (zs - apart) // 2,
    )
    middle = jnp.where(valid, jnp.mod(middle, zs), -1)
    loose = jnp.minimum(apart, zs - apart) <= 2 * reach - 2

    planes = jnp.arange(zs, dtype=jnp.int32)
    at = middle[None] == planes[:, None, None]
    load = jnp.sum(at.astype(jnp.float32), axis=2)
    total = jnp.sum(load, axis=0, keepdims=True)
    upto = (planes[None, :] <= planes[:, None]).astype(jnp.float32)
    excess = jnp.sum(upto[:, :, None] * (load * zs - total)[None], axis=1)
    centre = (jnp.max(excess, axis=0) + jnp.min(excess, axis=0)) * 0.5
    flow = jnp.floor((excess - centre) / zs + 0.5)
    rising = jnp.maximum(flow, 0.0)[:, :, None]
    falling = jnp.maximum(-jnp.roll(flow, 1, axis=0), 0.0)[:, :, None]

    movable = (at & loose[None]).astype(jnp.bfloat16)
    order = jnp.arange(zs * own, dtype=jnp.int32)
    earlier = (order[:, None] < order[None, :]).astype(jnp.bfloat16)
    rank = jnp.dot(
        movable.reshape(zs * columns, zs * own), earlier, preferred_element_type=jnp.float32
    ).reshape(zs, columns, zs * own)
    step = jnp.where(rank < rising, 1.0, jnp.where(rank < rising + falling, -1.0, 0.0))
    shift = jnp.sum(movable.astype(jnp.float32) * step, axis=0).astype(jnp.int32)
    middle = jnp.where(valid, jnp.mod(middle + shift, zs), -1)

    first_at = jnp.mod(first_plane - z + reach, zs) * plane_rows + jnp.mod(first, plane_rows)
    second_at = jnp.mod(second_plane - z + reach, zs) * plane_rows + jnp.mod(second, plane_rows)
    return middle, first_at * 4096 + second_at


def fill_slots(middle, packed, slots, z):
    here = middle == z
    order = jnp.arange(middle.shape[1], dtype=jnp.int32)
    earlier = (order[:, None] < order[None, :]).astype(jnp.bfloat16)
    rank = jnp.dot(here.astype(jnp.bfloat16), earlier, preferred_element_type=jnp.float32)
    rank = jnp.where(here, rank.astype(jnp.int32), -1)
    slot_ids = jnp.arange(slots, dtype=jnp.int32)
    taken = rank[:, None, :] == slot_ids[None, :, None]
    chosen = jnp.sum(jnp.where(taken, packed[:, None, :], 0), axis=2).reshape(-1)
    index = jnp.stack([chosen // 4096, chosen % 4096])
    used = jnp.minimum(jnp.sum(here.astype(jnp.int32), axis=1), slots)
    return index, used


def far_ring(near, axis, reach):
    size = lax.axis_size(axis)
    up, down = shifts(size)
    below, above = [], []
    from_below, from_above = near[0], near[-1]
    for step in range(reach + 1, size // 2 + 1):
        from_below = lax.ppermute(from_below, axis, up)
        below.append(from_below)
        if step < size - step:
            from_above = lax.ppermute(from_above, axis, down)
            above.append(from_above)
    return above + below[::-1]


def pick(table, digits_high, digits_low):
    rows, cols = table.shape
    hot = (digits_high[:, None] == jnp.arange(rows, dtype=jnp.int32)[None, :]).astype(jnp.bfloat16)
    digits = jnp.concatenate([table // 64, table % 64], axis=1).astype(jnp.bfloat16)
    found = jnp.dot(hot, digits, preferred_element_type=jnp.float32)
    mask = digits_low[:, None] == jnp.arange(cols, dtype=jnp.int32)[None, :]
    high = jnp.sum(jnp.where(mask, found[:, :cols], 0.0), axis=1)
    low = jnp.sum(jnp.where(mask, found[:, cols:], 0.0), axis=1)
    return (high * 64.0 + low).astype(jnp.int32)


def exchange_and_add(partial, group):
    columns = partial.reshape(group, -1, LAGS)
    shares = lax.all_to_all(columns, ("x", "y", "c"), 0, 0, tiled=True)
    return jnp.sum(shares.astype(jnp.float32), axis=0)


def body(spectra, station_pairs, station_home, block_lists):
    xs, ys, cs, zs = (lax.axis_size(n) for n in ("x", "y", "c", "z"))
    z, x = lax.axis_index("z"), lax.axis_index("x")
    owner = z * xs + x
    day = lax.axis_index("y") * cs + lax.axis_index("c")
    days = ys * cs
    column = x * days + day
    columns = xs * days
    rows = spectra.shape[1]
    freqs = spectra.shape[2] // 2
    share = freqs // xs
    scale = 1.0 / math.sqrt(spectra.shape[0] * days)
    pair_slots = station_pairs.shape[0]
    own = pair_slots // days
    plane_rows = rows * xs
    reach = zs // 4

    ends = jnp.concatenate([station_pairs[:, 0], station_pairs[:, 1]], axis=0)
    storage = pick(station_home.reshape(64, -1), ends // 64, ends % 64)
    source_block = storage // rows
    source_row = storage % rows
    wanted = lax.dynamic_index_in_dim(block_lists, owner, 0, keepdims=False)
    hot = (source_block[:, None] == jnp.arange(wanted.shape[0], dtype=jnp.int32)[None, :]).astype(
        jnp.bfloat16
    )
    candidates = jnp.dot(hot, wanted.astype(jnp.bfloat16), preferred_element_type=jnp.float32)
    listed = jnp.any(candidates == source_row.astype(jnp.float32)[:, None], axis=1)
    code = jnp.where(listed, storage, -1).reshape(1, 2 * pair_slots // LANES, LANES)
    code = jnp.broadcast_to(code, (zs * xs,) + code.shape[1:])

    real_part, imag_part = whiten(spectra[0])
    outbound = jnp.concatenate(
        [
            real_part.reshape(rows, xs, share // LANES, LANES),
            imag_part.reshape(rows, xs, share // LANES, LANES),
        ],
        axis=2,
    ).transpose(1, 0, 2, 3)
    block = lax.all_to_all(outbound, "x", 0, 0, tiled=True).reshape(plane_rows, 8, LANES)
    block, code = lax.optimization_barrier((block, code))
    codes = lax.all_to_all(code, ("z", "x"), 0, 0, tiled=True)
    basis = basis_slice(x * share, share, freqs)
    planes = jnp.arange(zs, dtype=jnp.int32)
    slots, returned = own + own // 4, own // 2
    slot_ids = jnp.arange(slots, dtype=jnp.int32)

    def place(codes):
        def first_branch(codes):
            return place_pairs(codes, zs, xs, days, own, plane_rows, z)

        def second_branch(codes):
            none = jnp.full((columns, zs * own), -1, jnp.int32)
            return none, none

        return lax.cond(codes[0, 0, 0] >= -1, first_branch, second_branch, codes)

    near, codes, basis, placed = near_ring(block, "z", reach, codes, basis, place)
    middle, packed = placed

    def first_branch(middle, packed):
        return fill_slots(middle, packed, slots, z)

    def second_branch(middle, packed):
        return jnp.zeros((2, columns * slots), jnp.int32), jnp.zeros((columns,), jnp.int32)

    index, used = lax.cond(codes[0, 0, 0] >= -1, first_branch, second_branch, middle, packed)
    core = lax.axis_index("c")
    by_core = index.reshape(2, columns // cs, cs, slots)
    used_by_core = used.reshape(columns // cs, cs)

    def of_core(k):
        some = lax.dynamic_index_in_dim(by_core, k, 2, keepdims=False).reshape(2, -1)
        return some, lax.dynamic_index_in_dim(used_by_core, k, 1, keepdims=False)

    other_index, other_used = of_core(1 - core)
    own_index, own_used = of_core(core)
    for_other, table = correlate(other_index, other_used, near, basis)
    from_other = lax.ppermute(for_other, "c", [(0, 1), (1, 0)])
    for_own = correlate_again(own_index, own_used, table, basis)
    both = (for_own.astype(jnp.float32) + from_other.astype(jnp.float32)).astype(jnp.bfloat16)
    shares = lax.all_to_all(both.reshape(xs * ys, slots, LAGS), ("x", "y"), 0, 0, tiled=True)
    added = jnp.sum(shares.astype(jnp.float32), axis=0)

    middle_by_owner = middle.reshape(columns, zs, own)
    meets = jnp.sum(
        (middle_by_owner[None] == planes[:, None, None, None]).astype(jnp.float32), axis=3
    )
    crowded = (jnp.max(jnp.sum(meets, axis=2)) > slots) | (jnp.max(meets) > returned)

    mine = lax.dynamic_index_in_dim(meets, column, 1, keepdims=False)
    sent = lax.dynamic_index_in_dim(mine, z, 0, keepdims=False)
    begin = jnp.sum(jnp.where(planes[None, :] < planes[:, None], sent[None, :], 0.0), axis=1)
    places = begin.astype(jnp.int32)[:, None] + jnp.arange(returned, dtype=jnp.int32)[None, :]
    send = (places.reshape(-1)[:, None] == slot_ids[None, :]).astype(jnp.bfloat16)
    own_column = lax.dynamic_index_in_dim(middle_by_owner, column, 0, keepdims=False)
    own_middle = lax.dynamic_index_in_dim(own_column, z, 0, keepdims=False)
    ids = jnp.arange(own, dtype=jnp.int32)
    before = (own_middle[:, None] == own_middle[None, :]) & (ids[None, :] < ids[:, None])
    own_at = own_middle * returned + jnp.sum(before.astype(jnp.int32), axis=1)
    own_at = jnp.where(own_middle >= 0, own_at, -1)
    take = (own_at[:, None] == jnp.arange(zs * returned, dtype=jnp.int32)[None, :]).astype(
        jnp.bfloat16
    )
    leaving = jnp.dot(send, added.astype(jnp.bfloat16), preferred_element_type=jnp.bfloat16)
    arrived = lax.all_to_all(
        leaving.reshape(zs, returned, LAGS), "z", 0, 0, tiled=True
    ).reshape(zs * returned, LAGS)
    by_middle = jnp.dot(take, arrived, preferred_element_type=jnp.float32) * scale

    def by_owner(near, codes, by_middle):
        plane = lax.dynamic_slice_in_dim(codes.reshape(zs, xs, 2, pair_slots), z, 1, 0)
        plane_codes = plane[0].transpose(1, 0, 2).reshape(2, xs * pair_slots)
        plane_at = jnp.mod(plane_codes // plane_rows - z + reach, zs) * plane_rows
        plane_at = plane_at + jnp.mod(plane_codes, plane_rows)
        plane_index = jnp.where(plane_codes >= 0, plane_at, zs * plane_rows)
        blocks = near + far_ring(near, "z", reach)
        every = jnp.full((columns,), own, jnp.int32)
        return exchange_and_add(correlate(plane_index, every, blocks, basis)[0], columns) * scale

    return lax.cond(
        crowded, by_owner, lambda near, codes, by_middle: by_middle, near, codes, by_middle
    )


def solution(mesh):
    inner = Mesh(mesh.devices.reshape(16, 4, 4, 2), ("z", "x", "y", "c"))
    in_specs = (P(("y", "c"), ("z", "x"), None), P(("z", "x"), None), P(), P())
    out_specs = P(("z", "x", "y", "c"), None)
    return jax.shard_map(
        body, mesh=inner, in_specs=in_specs, out_specs=out_specs, check_vma=False
    )
```

```python
import functools
import math

import jax
import jax.numpy as jnp
from jax import lax
from jax.experimental import pallas as pl
from jax.experimental.pallas import tpu as pltpu
from jax.sharding import Mesh
from jax.sharding import PartitionSpec as P

HALF = 32
LAGS = 256
LANES = 128


def basis_slice(first, count, freqs):
    freq_index = first + jnp.arange(count, dtype=jnp.int32)
    lag_index = jnp.arange(LAGS, dtype=jnp.int32) - LAGS // 2
    phase_steps = jnp.mod(freq_index[:, None] * lag_index[None, :], 2 * freqs)
    angles = phase_steps.astype(jnp.float32) * (2.0 * math.pi / (2 * freqs))
    scaling = 1.0 / math.sqrt(freqs)
    return jnp.concatenate([jnp.cos(angles) * scaling, -jnp.sin(angles) * scaling], axis=0).astype(
        jnp.bfloat16
    )


def whiten(station_rows):
    row_count = station_rows.shape[0]
    freq_count = station_rows.shape[1] // 2
    real_part = station_rows[:, :freq_count]
    imag_part = station_rows[:, freq_count:]
    amplitude = jnp.sqrt(real_part * real_part + imag_part * imag_part)
    extended = jnp.concatenate(
        [amplitude[:, freq_count - LANES :], amplitude, amplitude[:, :LANES]], axis=1
    )
    tile_count = freq_count // LANES
    grouped = extended.reshape(row_count, tile_count + 2, LANES)
    windows = jnp.concatenate(
        [grouped[:, :tile_count], grouped[:, 1 : tile_count + 1], grouped[:, 2:]], axis=2
    )
    band_rows = jnp.arange(3 * LANES, dtype=jnp.int32)[:, None]
    band_cols = jnp.arange(LANES, dtype=jnp.int32)[None, :]
    band_matrix = (jnp.abs(band_rows - band_cols - LANES) <= HALF).astype(jnp.float32)
    running = jnp.einsum(
        "snu,uv->snv", windows, band_matrix, precision=lax.Precision.HIGHEST
    ).reshape(row_count, freq_count)
    denominator = running / (2 * HALF + 1) + 1e-05
    return (real_part / denominator).astype(jnp.bfloat16), (imag_part / denominator).astype(
        jnp.bfloat16
    )


def load_table(blocks, table, sems):
    count, block_rows = len(blocks), blocks[0].shape[0]
    copies = [
        pltpu.make_async_copy(
            blocks[k], table.at[pl.ds(k * block_rows, block_rows)], sems.at[k]
        )
        for k in range(count)
    ]
    for copy in copies:
        copy.start()
    zero_rows = table.shape[0] - count * block_rows
    table[pl.ds(count * block_rows, zero_rows)] = jnp.zeros((zero_rows, 8, LANES), table.dtype)
    return copies


def loading_kernel(count, index_ref, used_ref, *refs):
    blocks = refs[:count]
    basis_ref, out_ref, table, cross, sems = refs[count:]
    copies = load_table(blocks, table, sems)
    clear_rows(cross)
    for copy in copies:
        copy.wait()
    cross_and_contract(index_ref, used_ref, table, basis_ref, out_ref, cross)


def reusing_kernel(index_ref, used_ref, table, basis_ref, out_ref, cross):
    clear_rows(cross)
    cross_and_contract(index_ref, used_ref, table, basis_ref, out_ref, cross)


def clear_rows(cross):
    def clear(i, carry):
        cross[pl.ds(pl.multiple_of(i * 256, 256), 256), :] = jnp.zeros((256, LANES), jnp.float32)
        return carry

    lax.fori_loop(0, cross.shape[0] // 256, clear, 0)


def cross_and_contract(index_ref, used_ref, table, basis_ref, out_ref, cross):
    slot_count = out_ref.shape[0]
    columns = used_ref.shape[0]
    slots = slot_count // columns
    low = lax.broadcasted_iota(jnp.int32, (8, LANES), 0) < 4
    group = 8
    whole = slots // 32 * 32

    def one_pair(p):
        a = table[index_ref[0, p]].astype(jnp.float32)
        b = table[index_ref[1, p]].astype(jnp.float32)
        swapped_a = pltpu.roll(a, 4, 0)
        swapped_b = pltpu.roll(b, 4, 0)
        real_b = jnp.where(low, b, swapped_b)
        imag_b = jnp.where(low, swapped_b, -b)
        start = pl.multiple_of(p * 8, 8)
        cross[pl.ds(start, 8), :] = a * real_b + swapped_a * imag_b

    def one_column(column, carry):
        base = column * slots
        for u in range(whole):
            one_pair(base + u)

        def one_group(g, inner):
            for u in range(group):
                one_pair(base + whole + g * group + u)
            return inner

        extra = jnp.maximum(used_ref[column] - whole + group - 1, 0) // group
        lax.fori_loop(0, extra, one_group, 0)
        return carry

    lax.fori_loop(0, columns, one_column, 0)
    step = 128

    def one_dot(i, carry):
        start = pl.multiple_of(i * step * 8, step * 8)
        rows = jnp.concatenate(
            [
                cross[pl.ds(start + k, step, stride=8), :].astype(jnp.bfloat16)
                for k in range(8)
            ],
            axis=1,
        )
        product = jnp.dot(rows, basis_ref[...], preferred_element_type=jnp.float32)
        out_ref[pl.ds(pl.multiple_of(i * step, step), step), :] = product.astype(out_ref.dtype)
        return carry

    lax.fori_loop(0, slot_count // step, one_dot, 0)


def correlate(index, used, blocks, basis):
    count = len(blocks)
    block_rows = blocks[0].shape[0]
    slot_count = index.shape[1]
    vmem = pl.BlockSpec(memory_space=pltpu.VMEM)
    smem = pl.BlockSpec(memory_space=pltpu.SMEM)
    return pl.pallas_call(
        functools.partial(loading_kernel, count),
        out_shape=[
            jax.ShapeDtypeStruct((slot_count, LAGS), jnp.bfloat16),
            jax.ShapeDtypeStruct((count * block_rows + 8, 8, LANES), jnp.bfloat16),
        ],
        in_specs=[smem, smem] + [pl.BlockSpec(memory_space=pl.ANY)] * count + [vmem],
        out_specs=[vmem, vmem],
        scratch_shapes=[
            pltpu.VMEM((slot_count * 8, LANES), jnp.float32),
            pltpu.SemaphoreType.DMA((count,)),
        ],
        compiler_params=pltpu.CompilerParams(vmem_limit_bytes=40 * 1024 * 1024),
    )(index, used, *blocks, basis)


def correlate_again(index, used, table, basis):
    slot_count = index.shape[1]
    vmem = pl.BlockSpec(memory_space=pltpu.VMEM)
    smem = pl.BlockSpec(memory_space=pltpu.SMEM)
    return pl.pallas_call(
        reusing_kernel,
        out_shape=jax.ShapeDtypeStruct((slot_count, LAGS), jnp.bfloat16),
        in_specs=[smem, smem, vmem, vmem],
        out_specs=vmem,
        scratch_shapes=[pltpu.VMEM((slot_count * 8, LANES), jnp.float32)],
        compiler_params=pltpu.CompilerParams(vmem_limit_bytes=32 * 1024 * 1024),
        cost_estimate=pl.CostEstimate(
            flops=2 * slot_count * 8 * LANES * LAGS, bytes_accessed=8 << 20, transcendentals=0
        ),
    )(index, used, table, basis)


def shifts(size):
    up = [(i, (i + 1) % size) for i in range(size)]
    down = [(i, (i - 1) % size) for i in range(size)]
    return up, down


def near_ring(block, axis, reach, codes, basis, place):
    up, down = shifts(lax.axis_size(axis))
    below, above = [], []
    from_below = from_above = block
    placed = None
    for step in range(reach):
        if step == reach - 2:
            from_below, from_above, codes, basis = lax.optimization_barrier(
                (from_below, from_above, codes, basis)
            )
        if step == reach - 1:
            from_below, from_above, placed = lax.optimization_barrier(
                (from_below, from_above, place(codes))
            )
        from_below = lax.ppermute(from_below, axis, up)
        from_above = lax.ppermute(from_above, axis, down)
        below.append(from_below)
        above.append(from_above)
    return below[::-1] + [block] + above, codes, basis, placed


def place_pairs(codes, zs, xs, days, own, plane_rows, z):
    columns = xs * days
    reach = zs // 4
    codes = codes.reshape(zs, xs, 2, days, own).transpose(2, 1, 3, 0, 4)
    first, second = codes.reshape(2, columns, zs * own)
    valid = (first >= 0) & (second >= 0)
    first_plane, second_plane = first // plane_rows, second // plane_rows
    apart = jnp.mod(second_plane - first_plane, zs)
    middle = jnp.where(
        apart <= zs // 2,
        first_plane + apart // 2,
        second_plane + (zs - apart) // 2,
    )
    middle = jnp.where(valid, jnp.mod(middle, zs), -1)
    loose = jnp.minimum(apart, zs - apart) <= 2 * reach - 2

    planes = jnp.arange(zs, dtype=jnp.int32)
    at = middle[None] == planes[:, None, None]
    load = jnp.sum(at.astype(jnp.float32), axis=2)
    total = jnp.sum(load, axis=0, keepdims=True)
    upto = (planes[None, :] <= planes[:, None]).astype(jnp.float32)
    excess = jnp.sum(upto[:, :, None] * (load * zs - total)[None], axis=1)
    centre = (jnp.max(excess, axis=0) + jnp.min(excess, axis=0)) * 0.5
    flow = jnp.floor((excess - centre) / zs + 0.5)
    rising = jnp.maximum(flow, 0.0)[:, :, None]
    falling = jnp.maximum(-jnp.roll(flow, 1, axis=0), 0.0)[:, :, None]

    movable = (at & loose[None]).astype(jnp.bfloat16)
    order = jnp.arange(zs * own, dtype=jnp.int32)
    earlier = (order[:, None] < order[None, :]).astype(jnp.bfloat16)
    rank = jnp.dot(
        movable.reshape(zs * columns, zs * own), earlier, preferred_element_type=jnp.float32
    ).reshape(zs, columns, zs * own)
    step = jnp.where(rank < rising, 1.0, jnp.where(rank < rising + falling, -1.0, 0.0))
    shift = jnp.sum(movable.astype(jnp.float32) * step, axis=0).astype(jnp.int32)
    middle = jnp.where(valid, jnp.mod(middle + shift, zs), -1)

    first_at = jnp.mod(first_plane - z + reach, zs) * plane_rows + jnp.mod(first, plane_rows)
    second_at = jnp.mod(second_plane - z + reach, zs) * plane_rows + jnp.mod(second, plane_rows)
    return middle, first_at * 4096 + second_at


def fill_slots(middle, packed, slots, z):
    here = middle == z
    order = jnp.arange(middle.shape[1], dtype=jnp.int32)
    earlier = (order[:, None] < order[None, :]).astype(jnp.bfloat16)
    rank = jnp.dot(here.astype(jnp.bfloat16), earlier, preferred_element_type=jnp.float32)
    rank = jnp.where(here, rank.astype(jnp.int32), -1)
    slot_ids = jnp.arange(slots, dtype=jnp.int32)
    taken = rank[:, None, :] == slot_ids[None, :, None]
    chosen = jnp.sum(jnp.where(taken, packed[:, None, :], 0), axis=2).reshape(-1)
    index = jnp.stack([chosen // 4096, chosen % 4096])
    used = jnp.minimum(jnp.sum(here.astype(jnp.int32), axis=1), slots)
    return index, used


def far_ring(near, axis, reach):
    size = lax.axis_size(axis)
    up, down = shifts(size)
    below, above = [], []
    from_below, from_above = near[0], near[-1]
    for step in range(reach + 1, size // 2 + 1):
        from_below = lax.ppermute(from_below, axis, up)
        below.append(from_below)
        if step < size - step:
            from_above = lax.ppermute(from_above, axis, down)
            above.append(from_above)
    return above + below[::-1]


def pick(table, digits_high, digits_low):
    rows, cols = table.shape
    hot = (digits_high[:, None] == jnp.arange(rows, dtype=jnp.int32)[None, :]).astype(jnp.bfloat16)
    digits = jnp.concatenate([table // 64, table % 64], axis=1).astype(jnp.bfloat16)
    found = jnp.dot(hot, digits, preferred_element_type=jnp.float32)
    mask = digits_low[:, None] == jnp.arange(cols, dtype=jnp.int32)[None, :]
    high = jnp.sum(jnp.where(mask, found[:, :cols], 0.0), axis=1)
    low = jnp.sum(jnp.where(mask, found[:, cols:], 0.0), axis=1)
    return (high * 64.0 + low).astype(jnp.int32)


def exchange_and_add(partial, group):
    columns = partial.reshape(group, -1, LAGS)
    shares = lax.all_to_all(columns, ("x", "y", "c"), 0, 0, tiled=True)
    return jnp.sum(shares.astype(jnp.float32), axis=0)


def body(spectra, station_pairs, station_home, block_lists):
    xs, ys, cs, zs = (lax.axis_size(n) for n in ("x", "y", "c", "z"))
    z, x = lax.axis_index("z"), lax.axis_index("x")
    owner = z * xs + x
    day = lax.axis_index("y") * cs + lax.axis_index("c")
    days = ys * cs
    column = x * days + day
    columns = xs * days
    rows = spectra.shape[1]
    freqs = spectra.shape[2] // 2
    share = freqs // xs
    scale = 1.0 / math.sqrt(spectra.shape[0] * days)
    pair_slots = station_pairs.shape[0]
    own = pair_slots // days
    plane_rows = rows * xs
    reach = zs // 4

    ends = jnp.concatenate([station_pairs[:, 0], station_pairs[:, 1]], axis=0)
    storage = pick(station_home.reshape(64, -1), ends // 64, ends % 64)
    source_block = storage // rows
    source_row = storage % rows
    wanted = lax.dynamic_index_in_dim(block_lists, owner, 0, keepdims=False)
    hot = (source_block[:, None] == jnp.arange(wanted.shape[0], dtype=jnp.int32)[None, :]).astype(
        jnp.bfloat16
    )
    candidates = jnp.dot(hot, wanted.astype(jnp.bfloat16), preferred_element_type=jnp.float32)
    listed = jnp.any(candidates == source_row.astype(jnp.float32)[:, None], axis=1)
    code = jnp.where(listed, storage, -1).reshape(1, 2 * pair_slots // LANES, LANES)
    code = jnp.broadcast_to(code, (zs * xs,) + code.shape[1:])

    real_part, imag_part = whiten(spectra[0])
    outbound = jnp.concatenate(
        [
            real_part.reshape(rows, xs, share // LANES, LANES),
            imag_part.reshape(rows, xs, share // LANES, LANES),
        ],
        axis=2,
    ).transpose(1, 0, 2, 3)
    block = lax.all_to_all(outbound, "x", 0, 0, tiled=True).reshape(plane_rows, 8, LANES)
    block, code = lax.optimization_barrier((block, code))
    codes = lax.all_to_all(code, ("z", "x"), 0, 0, tiled=True)
    basis = basis_slice(x * share, share, freqs)
    planes = jnp.arange(zs, dtype=jnp.int32)
    slots, returned = own + own // 4, own // 2
    slot_ids = jnp.arange(slots, dtype=jnp.int32)

    def place(codes):
        def first_branch(codes):
            return place_pairs(codes, zs, xs, days, own, plane_rows, z)

        def second_branch(codes):
            none = jnp.full((columns, zs * own), -1, jnp.int32)
            return none, none

        return lax.cond(codes[0, 0, 0] >= -1, first_branch, second_branch, codes)

    near, codes, basis, placed = near_ring(block, "z", reach, codes, basis, place)
    middle, packed = placed

    def first_branch(middle, packed):
        return fill_slots(middle, packed, slots, z)

    def second_branch(middle, packed):
        return jnp.zeros((2, columns * slots), jnp.int32), jnp.zeros((columns,), jnp.int32)

    index, used = lax.cond(codes[0, 0, 0] >= -1, first_branch, second_branch, middle, packed)
    core = lax.axis_index("c")
    by_core = index.reshape(2, columns // cs, cs, slots)
    used_by_core = used.reshape(columns // cs, cs)

    def of_core(k):
        some = lax.dynamic_index_in_dim(by_core, k, 2, keepdims=False).reshape(2, -1)
        return some, lax.dynamic_index_in_dim(used_by_core, k, 1, keepdims=False)

    other_index, other_used = of_core(1 - core)
    own_index, own_used = of_core(core)
    for_other, table = correlate(other_index, other_used, near, basis)
    from_other = lax.ppermute(for_other, "c", [(0, 1), (1, 0)])
    for_own = correlate_again(own_index, own_used, table, basis)
    both = (for_own.astype(jnp.float32) + from_other.astype(jnp.float32)).astype(jnp.bfloat16)
    both, middle = lax.optimization_barrier((both, middle))
    shares = lax.all_to_all(both.reshape(xs * ys, slots, LAGS), ("x", "y"), 0, 0, tiled=True)
    added = jnp.sum(shares.astype(jnp.float32), axis=0)

    middle_by_owner = middle.reshape(columns, zs, own)
    meets = jnp.sum(
        (middle_by_owner[None] == planes[:, None, None, None]).astype(jnp.float32), axis=3
    )
    crowded = (jnp.max(jnp.sum(meets, axis=2)) > slots) | (jnp.max(meets) > returned)

    mine = lax.dynamic_index_in_dim(meets, column, 1, keepdims=False)
    sent = lax.dynamic_index_in_dim(mine, z, 0, keepdims=False)
    begin = jnp.sum(jnp.where(planes[None, :] < planes[:, None], sent[None, :], 0.0), axis=1)
    places = begin.astype(jnp.int32)[:, None] + jnp.arange(returned, dtype=jnp.int32)[None, :]
    send = (places.reshape(-1)[:, None] == slot_ids[None, :]).astype(jnp.bfloat16)
    own_column = lax.dynamic_index_in_dim(middle_by_owner, column, 0, keepdims=False)
    own_middle = lax.dynamic_index_in_dim(own_column, z, 0, keepdims=False)
    ids = jnp.arange(own, dtype=jnp.int32)
    before = (own_middle[:, None] == own_middle[None, :]) & (ids[None, :] < ids[:, None])
    own_at = own_middle * returned + jnp.sum(before.astype(jnp.int32), axis=1)
    own_at = jnp.where(own_middle >= 0, own_at, -1)
    take = (own_at[:, None] == jnp.arange(zs * returned, dtype=jnp.int32)[None, :]).astype(
        jnp.bfloat16
    )
    leaving = jnp.dot(send, added.astype(jnp.bfloat16), preferred_element_type=jnp.bfloat16)
    arrived = lax.all_to_all(
        leaving.reshape(zs, returned, LAGS), "z", 0, 0, tiled=True
    ).reshape(zs * returned, LAGS)
    by_middle = jnp.dot(take, arrived, preferred_element_type=jnp.float32) * scale

    def by_owner(near, codes, by_middle):
        plane = lax.dynamic_slice_in_dim(codes.reshape(zs, xs, 2, pair_slots), z, 1, 0)
        plane_codes = plane[0].transpose(1, 0, 2).reshape(2, xs * pair_slots)
        plane_at = jnp.mod(plane_codes // plane_rows - z + reach, zs) * plane_rows
        plane_at = plane_at + jnp.mod(plane_codes, plane_rows)
        plane_index = jnp.where(plane_codes >= 0, plane_at, zs * plane_rows)
        blocks = near + far_ring(near, "z", reach)
        every = jnp.full((columns,), own, jnp.int32)
        return exchange_and_add(correlate(plane_index, every, blocks, basis)[0], columns) * scale

    return lax.cond(
        crowded, by_owner, lambda near, codes, by_middle: by_middle, near, codes, by_middle
    )


def solution(mesh):
    inner = Mesh(mesh.devices.reshape(16, 4, 4, 2), ("z", "x", "y", "c"))
    in_specs = (P(("y", "c"), ("z", "x"), None), P(("z", "x"), None), P(), P())
    out_specs = P(("z", "x", "y", "c"), None)
    return jax.shard_map(
        body, mesh=inner, in_specs=in_specs, out_specs=out_specs, check_vma=False
    )
```
